32 devices in a mesh: groups: 2 (over y), seq: 16 (over z, x, core).
Axes of the slice: x: 2, y: 2, z: 4, core: 2. Of those that a mesh axis runs over, the one named last changes fastest.
Arguments:
- frames: bfloat16 [64, 32, 128, 128], P(('groups', 'seq')), parts along dimension 0, may hold values from -6 to 6
- w_spatial: bfloat16 [3, 3, 128, 128], replicated, may hold values from -0.1875 to 0.1875
- w_temporal: bfloat16 [2, 3, 128, 128], replicated, may hold values from -0.3125 to 0.3125
- dilations: int32 [2], replicated, may hold values from 1 to 16
- offsets: int32 [2, 3], replicated, may hold values from 0 to 3
- cotangent: bfloat16 [64, 1024, 128], P('groups', 'seq'), parts along dimension 0, may hold values from -0.011962891 to 0.011962891
Outputs:
- features: bfloat16 [64, 1024, 128], P('groups', 'seq'), parts along dimension 0
- grad_spatial: float32 [6, 3, 128, 128], P('groups'), parts along dimension 0
- grad_temporal: float32 [4, 3, 128, 128], P('groups'), parts along dimension 0
The draws below stay inside these ranges and needn't reach their ends.
There are 2 independent parts, one for each index of `groups`. The reference program is written for one: setup_inputs(seed, part) draws one part's arguments, and reference() takes and returns one part's arrays. A program takes and returns all parts, laid end to end along the dimension named above; an argument that names none is the same for every part. Nothing has to cross between parts.
All inputs are finite; a program needn't handle non-finite values.
Results may differ from the reference program's by a relative error of at most 0.0067.
Values may be sent and summed in bfloat16 or wider, within the bound.
A program may use at most 64 MiB of HBM per device.

```python
import jax
import jax.numpy as jnp
from jax import lax

C = 128
W_IN = 128
H_IN = 32
LAYERS = 2
KT = 3
PIX = 1024
FRAMES = 32
N_SEQ = 16


def draw_dilations(key, part):
    first, second = jax.random.split(jax.random.fold_in(key, 11))
    values = jax.random.randint(first, (LAYERS,), 1, 17)
    where_top = jax.random.randint(second, (), 0, LAYERS)
    return jnp.where(jnp.arange(LAYERS) == where_top, 16, values).astype(jnp.int32)


def draw_offsets(key, part):
    first, second = jax.random.split(jax.random.fold_in(key, 23))
    values = jax.random.randint(first, (LAYERS * KT,), 0, 4)
    where_top = jax.random.randint(second, (), 0, LAYERS * KT)
    values = jnp.where(jnp.arange(LAYERS * KT) == where_top, 3, values)
    return values.reshape(LAYERS, KT).astype(jnp.int32)


def block_scale(own_key, dims, pieces, least, top_value):
    level = 1.0
    for axis_at, shards_of in pieces:
        steps = jax.random.uniform(jax.random.fold_in(jax.random.fold_in(own_key, 6), axis_at), (shards_of,), jnp.float32, least / len(pieces), top_value / len(pieces))
        level = level * jnp.repeat(jnp.exp(steps), dims[axis_at] // shards_of).reshape((-1,) + (1,) * (len(dims) - 1 - axis_at))
    return level


def gaussian(own_key, dims, deviation, most, cuts=(), kind=jnp.bfloat16):
    loudness = block_scale(own_key, dims, cuts, -0.22, 0.18) if cuts else 1.0
    result = jax.random.normal(own_key, dims, jnp.float32) * deviation * loudness
    return jnp.minimum(jnp.maximum(result, -most), most).astype(kind)


def setup_inputs(seed: int = 0, part: int = 0) -> dict:
    keys = jax.random.split(jax.random.key(seed), 7)
    own_keys = jax.random.split(jax.random.fold_in(keys[6], part), 7)
    frames = gaussian(own_keys[0], (FRAMES, H_IN, W_IN, C), 1.0, 6.0, ((0, 16),))
    w_spatial = gaussian(keys[1], (3, 3, C, C), (9 * C) ** -0.5, 0.1875)
    w_temporal = gaussian(keys[2], (LAYERS, KT, C, C), (KT * C) ** -0.5, 0.3125)
    dilations = draw_dilations(jax.random.fold_in(keys[6], 71), part)
    offsets = draw_offsets(jax.random.fold_in(keys[6], 71), part)
    cotangent = gaussian(own_keys[5], (FRAMES, PIX, C), 0.002, 0.011962891, ((1, 16),))
    return {"frames": frames, "w_spatial": w_spatial, "w_temporal": w_temporal, "dilations": dilations, "offsets": offsets, "cotangent": cotangent}


def padded_view(frame):
    height, width, channels = frame.shape
    padded = jnp.pad(frame, ((1, 1), (1, 1), (0, 0)))
    return padded.reshape(height // 2 + 1, 2, width // 2 + 1, 2, channels)

def window(view, row_tap, col_tap):
    out_rows = view.shape[0] - 1
    out_cols = view.shape[2] - 1
    return view[row_tap // 2:row_tap // 2 + out_rows, row_tap % 2, col_tap // 2:col_tap // 2 + out_cols, col_tap % 2, :]

def spatial_frame(frame, w_spatial):
    view = padded_view(frame)
    channels = frame.shape[2]
    total = jnp.zeros((view.shape[0] - 1) * (view.shape[2] - 1) * 0 + (view.shape[0] - 1) * (view.shape[2] - 1), jnp.float32)
    total = jnp.zeros(((view.shape[0] - 1) * (view.shape[2] - 1), channels), jnp.float32)
    for row_tap in range(3):
        for col_tap in range(3):
            patch = window(view, row_tap, col_tap).reshape(-1, channels)
            total = total + jnp.dot(patch, w_spatial[row_tap, col_tap], preferred_element_type=jnp.float32)
    return total.astype(jnp.bfloat16)

def spatial_frame_grad(frame, back):
    view = padded_view(frame)
    channels = frame.shape[2]
    rows = []
    for row_tap in range(3):
        cols = []
        for col_tap in range(3):
            patch = window(view, row_tap, col_tap).reshape(-1, channels)
            cols.append(lax.dot_general(patch, back, (((0,), (0,)), ((), ())), preferred_element_type=jnp.float32))
        rows.append(jnp.stack(cols))
    return jnp.stack(rows)

def delayed(values, delay):
    length = values.shape[0]
    delay = jnp.minimum(delay, length).astype(jnp.int32)
    joined = jnp.concatenate([jnp.zeros_like(values), values], 0)
    return lax.dynamic_slice_in_dim(joined, (length - delay).astype(jnp.int32), length, 0)

def advanced(values, delay):
    length = values.shape[0]
    delay = jnp.minimum(delay, length).astype(jnp.int32)
    joined = jnp.concatenate([values, jnp.zeros_like(values)], 0)
    return lax.dynamic_slice_in_dim(joined, delay, length, 0)

def temporal_block(start, cot_block, w_temporal, delays):
    length, pixels, channels = start.shape
    layer_count, tap_count = (w_temporal.shape[0], w_temporal.shape[1])
    states = [start]
    activations = []
    for layer in range(layer_count):
        state = states[-1]
        total = jnp.zeros((length * pixels, channels), jnp.float32)
        for tap in range(tap_count):
            moved = delayed(state, delays[layer, tap]).reshape(-1, channels)
            total = total + jnp.dot(moved, w_temporal[layer, tap], preferred_element_type=jnp.float32)
        activ = jnp.tanh(total).reshape(length, pixels, channels)
        activations.append(activ)
        states.append((state.astype(jnp.float32) + activ).astype(jnp.bfloat16))
    grad_state = cot_block.astype(jnp.float32)
    grads = [None] * layer_count
    for layer in reversed(range(layer_count)):
        activ = activations[layer]
        dz_flat = (grad_state * (1.0 - activ * activ)).astype(jnp.bfloat16).reshape(-1, channels)
        layer_grads = []
        for tap in range(tap_count):
            moved = delayed(states[layer], delays[layer, tap]).reshape(-1, channels)
            layer_grads.append(lax.dot_general(moved, dz_flat, (((0,), (0,)), ((), ())), preferred_element_type=jnp.float32))
            backward = jnp.dot(dz_flat, w_temporal[layer, tap].T, preferred_element_type=jnp.float32)
            grad_state = grad_state + advanced(backward.reshape(length, pixels, channels), delays[layer, tap])
        grads[layer] = jnp.stack(layer_grads)
    return (states[-1], grad_state.astype(jnp.bfloat16), jnp.stack(grads))

def reference(frames, w_spatial, w_temporal, dilations, offsets, cotangent):
    delays = (offsets * dilations[:, None]).astype(jnp.int32)
    spatial = lax.map(lambda frame: spatial_frame(frame, w_spatial), frames)
    pixels_dev = PIX // N_SEQ
    blocked = spatial.reshape(FRAMES, N_SEQ, pixels_dev, C).transpose(1, 0, 2, 3)
    cot_blocks = cotangent.reshape(FRAMES, N_SEQ, pixels_dev, C).transpose(1, 0, 2, 3)

    def block_step(carry, pair):
        final, back, grads = temporal_block(pair[0], pair[1], w_temporal, delays)
        return (carry + grads, (final, back))
    grad_temporal, outputs = lax.scan(block_step, jnp.zeros((LAYERS, KT, C, C), jnp.float32), (blocked, cot_blocks))
    features = outputs[0].transpose(1, 0, 2, 3).reshape(FRAMES, PIX, C)
    back_maps = outputs[1].transpose(1, 0, 2, 3).reshape(FRAMES, PIX, C)

    def frame_step(carry, pair):
        return (carry + spatial_frame_grad(pair[0], pair[1]), None)
    grad_spatial, unused = lax.scan(frame_step, jnp.zeros((3, 3, C, C), jnp.float32), (frames, back_maps))
    return (features, grad_spatial, grad_temporal)
```

```python
import functools

import jax
import jax.numpy as jnp
from jax import lax
from jax.experimental import pallas as pl
from jax.experimental.pallas import tpu as pltpu
from jax.sharding import PartitionSpec as P

BF16 = jnp.bfloat16
F32 = jnp.float32
MESH = pl.DeviceIdType.MESH


def kernel(
    n,
    dil_ref,
    off_ref,
    frames_ref,
    ws_ref,
    wt_ref,
    cot_ref,
    feat_ref,
    gs_ref,
    gt_ref,
    tmp,
    xcols,
    spat,
    land,
    s0,
    s1,
    act0,
    d1,
    d0,
    maps,
    back,
    wback,
    grads,
    pair_out,
    pair_in,
    chip_out,
    chip_in,
    own,
    gathered,
    send1,
    recv1,
    send2,
    recv2,
    ar_send,
    ar_recv,
):
    me = lax.axis_index("seq")
    per, height, width, ch = frames_ref.shape
    length, pix, _ = cot_ref.shape
    layers, taps = off_ref.shape
    out_h, out_w = height // 2, width // 2
    blocks = out_w // pix
    q_count = recv2.shape[0]
    q_rows = out_h // q_count
    q_devs = q_rows * blocks
    t_count = recv1.shape[0]
    t_len = length // t_count
    t_devs = t_len // per
    chips = n // 2
    core = lax.rem(me, 2)
    chip = me // 2
    partner = me + 1 - 2 * core
    sp_rows = gs_ref.shape[0]
    tap_rows = taps * ch

    def flat(x):
        if pix % 16 == 0:
            return x.reshape(-1, ch)
        return x.astype(F32).reshape(-1, ch).astype(BF16)

    def unflat(x):
        return x.reshape(-1, pix, ch)

    def delay(layer, tap):
        return jnp.minimum(off_ref[layer, tap] * dil_ref[layer], length)

    barrier = pltpu.get_barrier_semaphore()

    def greet(s, carry):
        pl.semaphore_signal(
            barrier, inc=1, device_id={"seq": lax.rem(me + s, n)}, device_id_type=MESH
        )
        return carry

    lax.fori_loop(1, n, greet, 0)

    group = tmp.shape[0]
    for g in range(group):
        tmp[g, 0:8, :] = jnp.zeros((8, ch), F32)
    for f in range(per):
        xcols[f, 0, 0] = jnp.zeros((out_w, 3 * ch), BF16)

    def spread(step, carry):
        for f in range(per):
            for g in range(group):
                r = step * group + g
                tmp[g, 8 : 8 + width, :] = frames_ref[f, r].astype(F32)
            for g in range(group):
                half = (g + 1) // 2
                row = step * (group // 2) + half
                for b in range(3):
                    xcols[f, row, (g + 1) % 2, :, b * ch : (b + 1) * ch] = tmp[
                        g, pl.ds(7 + b, out_w, stride=2), :
                    ].astype(BF16)
        return carry

    lax.fori_loop(0, height // group, spread, 0)

    def patches(f, i0, count):
        parts = [
            xcols[f, pl.ds(i0, count), 0],
            xcols[f, pl.ds(i0, count), 1],
            xcols[f, pl.ds(i0 + 1, count), 0],
        ]
        return jnp.concatenate([p.reshape(count * out_w, 3 * ch) for p in parts], axis=1)

    pl.semaphore_wait(barrier, n - 1)

    my_q = me // q_devs

    def conv(s, carry):
        q = lax.rem(my_q + 1 + s, q_count)
        for f in range(per):
            out = jnp.dot(
                patches(f, q * q_rows, q_rows), ws_ref[...], preferred_element_type=F32
            )
            spat[pl.ds(q * q_devs, q_devs), f] = unflat(out).astype(BF16)

        def send(k, c):
            j = q * q_devs + lax.rem(me + k, q_devs)

            @pl.when(j != me)
            def _():
                pltpu.make_async_remote_copy(
                    src_ref=spat.at[j],
                    dst_ref=land.at[pl.ds(me * per, per)],
                    send_sem=send1,
                    recv_sem=recv1.at[me // t_devs],
                    device_id={"seq": j},
                    device_id_type=MESH,
                ).start()

            @pl.when(j == me)
            def _():
                pltpu.make_async_copy(
                    spat.at[me],
                    land.at[pl.ds(me * per, per)],
                    recv1.at[me // t_devs],
                ).start()

            return c

        lax.fori_loop(0, q_devs, send, 0)
        return carry

    lax.fori_loop(0, q_count, conv, 0)

    def clear(t, carry):
        zero = jnp.zeros((t_len, pix, ch), BF16)
        s0[pl.ds(t * t_len, t_len)] = zero
        s1[pl.ds(t * t_len, t_len)] = zero
        d1[pl.ds(length + t * t_len, t_len)] = zero
        d0[pl.ds(length + t * t_len, t_len)] = zero
        return carry

    lax.fori_loop(0, t_count, clear, 0)
    grads[...] = jnp.zeros_like(grads)
    for layer in range(layers):
        for tap in range(taps):
            w = wt_ref[layer, tap * ch : (tap + 1) * ch, :]
            wback[layer, tap * ch : (tap + 1) * ch, :] = w.astype(F32).T.astype(BF16)

    def lagged(ref, layer, t0):
        return jnp.concatenate(
            [flat(ref[pl.ds(length + t0 - delay(layer, k), t_len)]) for k in range(taps)], axis=1
        )

    def led(ref, layer, t0):
        return jnp.concatenate(
            [flat(ref[pl.ds(t0 + delay(layer, k), t_len)]) for k in range(taps)], axis=1
        )

    def outer(x, y):
        return lax.dot_general(x, y, (((0,), (0,)), ((), ())), preferred_element_type=F32)

    base0 = sp_rows
    base1 = sp_rows + tap_rows

    def forward(t, carry):
        t0 = t * t_len
        arrived = land.at[pl.ds(t0, t_len)]
        pltpu.make_async_copy(arrived, arrived, recv1.at[t]).wait()
        state = land[pl.ds(t0, t_len)]
        s0[pl.ds(length + t0, t_len)] = state
        z = jnp.dot(lagged(s0, 0, t0), wt_ref[0], preferred_element_type=F32)
        act = unflat(jnp.tanh(z))
        act0[pl.ds(t0, t_len)] = act
        state = (state.astype(F32) + act).astype(BF16)
        s1[pl.ds(length + t0, t_len)] = state
        moved = lagged(s1, 1, t0)
        act = unflat(jnp.tanh(jnp.dot(moved, wt_ref[1], preferred_element_type=F32)))
        feat_ref[pl.ds(t0, t_len)] = (state.astype(F32) + act).astype(BF16)
        dz = (cot_ref[pl.ds(t0, t_len)].astype(F32) * (1.0 - act * act)).astype(BF16)
        d1[pl.ds(t0, t_len)] = dz
        grads[pl.ds(base1, tap_rows), :] += outer(moved, flat(dz))
        return carry

    lax.fori_loop(0, t_count, forward, 0)

    def backward(s, carry):
        t = t_count - 1 - s
        t0 = t * t_len
        state = cot_ref[pl.ds(t0, t_len)].astype(F32) + unflat(
            jnp.dot(led(d1, 1, t0), wback[1], preferred_element_type=F32)
        )
        act = act0[pl.ds(t0, t_len)]
        dz = (state * (1.0 - act * act)).astype(BF16)
        d0[pl.ds(t0, t_len)] = dz
        state = state + unflat(jnp.dot(led(d0, 0, t0), wback[0], preferred_element_type=F32))
        maps[pl.ds(t0, t_len)] = state.astype(BF16)

        def send(k, c):
            j = t * t_devs + lax.rem(me + k, t_devs)

            @pl.when(j != me)
            def _():
                pltpu.make_async_remote_copy(
                    src_ref=maps.at[pl.ds(j * per, per)],
                    dst_ref=back.at[me],
                    send_sem=send2,
                    recv_sem=recv2.at[me // q_devs],
                    device_id={"seq": j},
                    device_id_type=MESH,
                ).start()

            @pl.when(j == me)
            def _():
                pltpu.make_async_copy(
                    maps.at[pl.ds(me * per, per)], back.at[me], recv2.at[me // q_devs]
                ).start()

            return c

        lax.fori_loop(0, t_devs, send, 0)
        grads[pl.ds(base0, tap_rows), :] += outer(lagged(s0, 0, t0), flat(dz))
        return carry

    lax.fori_loop(0, t_count, backward, 0)

    def conv_grad(s, carry):
        q = lax.rem(my_q + s, q_count)
        arrived = back.at[pl.ds(q * q_devs, q_devs)]
        pltpu.make_async_copy(arrived, arrived, recv2.at[q]).wait()
        x = jnp.concatenate([patches(f, q * q_rows, q_rows) for f in range(per)], axis=0)
        g = jnp.concatenate([flat(back[pl.ds(q * q_devs, q_devs), f]) for f in range(per)], axis=0)
        grads[0:sp_rows, :] += outer(x, g)
        return carry

    lax.fori_loop(0, q_count, conv_grad, 0)

    rows = pair_out.shape[2]
    half = chips * rows

    def as_pieces(x):
        return x.reshape(chips, rows, ch)

    for c in range(2):
        pair_out[c] = as_pieces(grads[c * half : (c + 1) * half, :].astype(BF16))
    pair = pltpu.make_async_remote_copy(
        src_ref=pair_out.at[1 - core],
        dst_ref=pair_in,
        send_sem=ar_send.at[0],
        recv_sem=ar_recv.at[0],
        device_id={"seq": partner},
        device_id_type=MESH,
    )
    pair.start()
    mine = as_pieces(grads[pl.ds(pl.multiple_of(core * half, half), half), :])
    pair.wait_recv()
    chip_out[...] = (mine + pair_in[...].astype(F32)).astype(BF16)

    def scatter(k, carry):
        c = lax.rem(chip + k, chips)
        pltpu.make_async_remote_copy(
            src_ref=chip_out.at[c],
            dst_ref=chip_in.at[chip],
            send_sem=ar_send.at[1],
            recv_sem=ar_recv.at[1],
            device_id={"seq": 2 * c + core},
            device_id_type=MESH,
        ).start()
        return carry

    pltpu.make_async_copy(chip_out.at[chip], chip_in.at[chip], ar_recv.at[1]).start()
    lax.fori_loop(1, chips, scatter, 0)
    pltpu.make_async_copy(chip_in, chip_in, ar_recv.at[1]).wait()
    own[...] = jnp.sum(chip_in[...].astype(F32), axis=0).astype(BF16)

    def gather(k, carry):
        c = lax.rem(chip + k, chips)
        pltpu.make_async_remote_copy(
            src_ref=own,
            dst_ref=gathered.at[core, chip],
            send_sem=ar_send.at[2],
            recv_sem=ar_recv.at[2],
            device_id={"seq": 2 * c + core},
            device_id_type=MESH,
        ).start()
        return carry

    pltpu.make_async_copy(own, gathered.at[core, chip], ar_recv.at[2]).start()
    lax.fori_loop(1, chips, gather, 0)
    mine_all = gathered.at[core]
    pltpu.make_async_copy(mine_all, mine_all, ar_recv.at[2]).wait()
    swap = pltpu.make_async_remote_copy(
        src_ref=gathered.at[core],
        dst_ref=gathered.at[core],
        send_sem=ar_send.at[3],
        recv_sem=ar_recv.at[3],
        device_id={"seq": partner},
        device_id_type=MESH,
    )
    swap.start()
    swap.wait_recv()
    total = gathered[...].astype(F32).reshape(2 * half, ch)
    gs_ref[...] = total[:sp_rows]
    gt_ref[...] = total[sp_rows : sp_rows + gt_ref.shape[0]]

    pair.wait_send()
    swap.wait_send()
    most = spat.at[pl.ds(0, n - 1)]
    pltpu.make_async_copy(most, most, send1).wait()
    most = back.at[pl.ds(0, n - 1)]
    pltpu.make_async_copy(most, most, send2).wait()
    most = chip_out.at[pl.ds(0, chips - 1)]
    pltpu.make_async_copy(most, most, ar_send.at[1]).wait()
    pltpu.make_async_copy(most, most, ar_send.at[2]).wait()


def local(n, frames, w_spatial, w_temporal, dilations, offsets, cotangent):
    per, height, width, ch = frames.shape
    length, pix, _ = cotangent.shape
    layers, taps = offsets.shape
    out_h, out_w = height // 2, width // 2
    sp_rows, tp_rows = 9 * ch, layers * taps * ch
    unit = 16 * n
    rows = -(-(sp_rows + tp_rows) // unit) * 16
    chips = n // 2
    t_count = max(1, length * pix // 512)
    q_count = 4
    vmem = pl.BlockSpec(memory_space=pltpu.VMEM)
    smem = pl.BlockSpec(memory_space=pltpu.SMEM)
    dma = pltpu.SemaphoreType.DMA
    features, grad_spatial, grad_temporal = pl.pallas_call(
        functools.partial(kernel, n),
        out_shape=(
            jax.ShapeDtypeStruct((length, pix, ch), BF16),
            jax.ShapeDtypeStruct((sp_rows, ch), F32),
            jax.ShapeDtypeStruct((tp_rows, ch), F32),
        ),
        in_specs=[smem, smem, vmem, vmem, vmem, vmem],
        out_specs=(vmem, vmem, vmem),
        scratch_shapes=[
            pltpu.VMEM((8, width + 8, ch), F32),
            pltpu.VMEM((per, out_h + 1, 2, out_w, 3 * ch), BF16),
            pltpu.VMEM((n, per, pix, ch), BF16),
            pltpu.VMEM((length, pix, ch), BF16),
            pltpu.VMEM((2 * length, pix, ch), BF16),
            pltpu.VMEM((2 * length, pix, ch), BF16),
            pltpu.VMEM((length, pix, ch), F32),
            pltpu.VMEM((2 * length, pix, ch), BF16),
            pltpu.VMEM((2 * length, pix, ch), BF16),
            pltpu.VMEM((length, pix, ch), BF16),
            pltpu.VMEM((n, per, pix, ch), BF16),
            pltpu.VMEM((layers, taps * ch, ch), BF16),
            pltpu.VMEM((n * rows, ch), F32),
            pltpu.VMEM((2, chips, rows, ch), BF16),
            pltpu.VMEM((chips, rows, ch), BF16),
            pltpu.VMEM((chips, rows, ch), BF16),
            pltpu.VMEM((chips, rows, ch), BF16),
            pltpu.VMEM((rows, ch), BF16),
            pltpu.VMEM((2, chips, rows, ch), BF16),
            dma,
            dma((t_count,)),
            dma,
            dma((q_count,)),
            dma((4,)),
            dma((4,)),
        ],
        compiler_params=pltpu.CompilerParams(
            collective_id=0, has_side_effects=True, vmem_limit_bytes=48 * 1024 * 1024
        ),
        cost_estimate=pl.CostEstimate(
            flops=2 * (length * pix) * ch * ch * 36, bytes_accessed=8 << 20, transcendentals=0
        ),
    )(
        dilations,
        offsets,
        frames,
        w_spatial.reshape(sp_rows, ch),
        w_temporal.reshape(layers, taps * ch, ch),
        cotangent,
    )
    return (
        features,
        grad_spatial.reshape(3, 3, ch, ch),
        grad_temporal.reshape(layers, taps, ch, ch),
    )


def solution(mesh):
    in_specs = (
        P(("groups", "seq"), None, None, None),
        P(),
        P(),
        P(),
        P(),
        P("groups", "seq", None),
    )
    out_specs = (
        P("groups", "seq", None),
        P("groups", None, None, None),
        P("groups", None, None, None),
    )
    return jax.shard_map(
        functools.partial(local, mesh.shape["seq"]),
        mesh=mesh,
        in_specs=in_specs,
        out_specs=out_specs,
        check_vma=False,
    )
```

```python
import functools

import jax
import jax.numpy as jnp
from jax import lax
from jax.experimental import pallas as pl
from jax.experimental.pallas import tpu as pltpu
from jax.sharding import PartitionSpec as P

BF16 = jnp.bfloat16
F32 = jnp.float32
MESH = pl.DeviceIdType.MESH
PARTS = 4


def remote(src, dst, send, recv, to):
    return pltpu.make_async_remote_copy(
        src_ref=src,
        dst_ref=dst,
        send_sem=send,
        recv_sem=recv,
        device_id={"seq": to},
        device_id_type=MESH,
    )


def drain(ref, sem):
    pltpu.make_async_copy(ref, ref, sem).wait()


class Reduce:
    def __init__(self, n, out, total, pair_out, pair_in, chip_out, chip_in, own, gathered, send, recv):
        self.total, self.pair_out, self.pair_in = total, pair_out, pair_in
        self.chip_out, self.chip_in, self.own = chip_out, chip_in, own
        self.gathered, self.send, self.recv, self.out = gathered, send, recv, out
        self.chips = n // 2
        me = lax.axis_index("seq")
        self.core, self.chip = lax.rem(me, 2), me // 2
        self.partner = me + 1 - 2 * self.core
        self.rows, self.ch = own.shape
        self.half = self.chips * self.rows
        self.pair = remote(
            pair_out.at[1 - self.core], pair_in, send.at[0], recv.at[0], self.partner
        )
        self.swap = remote(
            gathered.at[self.core], gathered.at[self.core], send.at[3], recv.at[3], self.partner
        )

    def pieces(self, x):
        return x.reshape(self.chips, self.rows, self.ch)

    def chips_loop(self, src_of, dst, hop):
        def step(k, carry):
            c = lax.rem(self.chip + k, self.chips)
            remote(
                src_of(c), dst, self.send.at[hop], self.recv.at[hop], 2 * c + self.core
            ).start()
            return carry

        lax.fori_loop(1, self.chips, step, 0)

    def start(self):
        for c in range(2):
            part = self.total[c * self.half : (c + 1) * self.half, :]
            self.pair_out[c] = self.pieces(part.astype(BF16))
        self.pair.start()

    def scatter(self):
        at = pl.multiple_of(self.core * self.half, self.half)
        mine = self.pieces(self.total[pl.ds(at, self.half), :])
        self.pair.wait_recv()
        self.chip_out[...] = (mine + self.pair_in[...].astype(F32)).astype(BF16)
        dst = self.chip_in.at[self.chip]
        self.chips_loop(lambda c: self.chip_out.at[c], dst, 1)
        pltpu.make_async_copy(self.chip_out.at[self.chip], dst, self.recv.at[1]).start()

    def gather(self):
        drain(self.chip_in, self.recv.at[1])
        self.own[...] = jnp.sum(self.chip_in[...].astype(F32), axis=0).astype(BF16)
        dst = self.gathered.at[self.core, self.chip]
        self.chips_loop(lambda c: self.own, dst, 2)
        pltpu.make_async_copy(self.own, dst, self.recv.at[2]).start()

    def exchange(self):
        drain(self.gathered.at[self.core], self.recv.at[2])
        self.swap.start()
        self.store(self.core).start()

    def finish(self):
        self.swap.wait_recv()
        self.store(1 - self.core).start()

    def store(self, side):
        return pltpu.make_async_copy(self.gathered.at[side], self.out.at[side], self.recv.at[4])

    def sent(self):
        self.pair.wait_send()
        self.swap.wait_send()
        most = self.chip_out.at[pl.ds(0, self.chips - 1)]
        drain(most, self.send.at[1])
        drain(most, self.send.at[2])
        drain(self.gathered, self.recv.at[4])


def kernel(
    n,
    dil_ref,
    off_ref,
    frames_hbm,
    ws_hbm,
    wt_hbm,
    cot_hbm,
    feat_hbm,
    gs_hbm,
    gt_hbm,
    feat_ref,
    frames_ref,
    ws_ref,
    wt_ref,
    cot_ref,
    tmp,
    xcols,
    spat,
    land,
    s0,
    s1,
    act0,
    d1,
    d0,
    maps,
    back,
    wback,
    sum_s,
    sum_t,
    *rest,
):
    red_s = Reduce(n, gs_hbm, sum_s, *rest[0:8])
    red_t = Reduce(n, gt_hbm, sum_t, *rest[8:16])
    send1, recv1, send2, recv2, load = rest[16:]
    me = lax.axis_index("seq")
    per, height, width, ch = frames_ref.shape
    length, pix, _ = cot_ref.shape
    layers, taps = off_ref.shape
    parts, _, _, pp, _ = spat.shape
    out_h, out_w = height // 2, width // 2
    cw = out_w // parts
    q_count = 4
    q_rows = out_h // q_count
    q_devs = n // q_count
    g_count = max(1, per * out_h * cw // 512)
    g_rows, g_devs = out_h // g_count, n // g_count
    t_count = max(1, length * pp // 512)
    t_len = length // t_count
    sp_rows = ws_ref.shape[0]
    tap_rows = taps * ch

    fetch = [
        pltpu.make_async_copy(frames_hbm.at[f], frames_ref.at[f], load.at[f]) for f in range(per)
    ]
    fetch += [
        pltpu.make_async_copy(a, b, load.at[per + i])
        for i, (a, b) in enumerate([(ws_hbm, ws_ref), (wt_hbm, wt_ref), (cot_hbm, cot_ref)])
    ]
    for copy in fetch:
        copy.start()

    def flat(x):
        if pp % 16 == 0:
            return x.reshape(-1, x.shape[-1])
        return x.astype(F32).reshape(-1, x.shape[-1]).astype(BF16)

    def unflat(x):
        return x.reshape(-1, pp, ch)

    def delay(layer, tap):
        return jnp.minimum(off_ref[layer, tap] * dil_ref[layer], length)

    barrier = pltpu.get_barrier_semaphore()

    def greet(s, carry):
        pl.semaphore_signal(
            barrier, inc=1, device_id={"seq": lax.rem(me + s, n)}, device_id_type=MESH
        )
        return carry

    lax.fori_loop(1, n, greet, 0)

    group = tmp.shape[0]
    for g in range(group):
        tmp[g, 0:8, :] = jnp.zeros((8, ch), F32)
    for f in range(per):
        xcols[f, 0, 0] = jnp.zeros((parts, cw, 3 * ch), BF16)

    for f in range(per):
        fetch[f].wait()

        def spread(step, carry):
            for g in range(group):
                tmp[g, 8 : 8 + width, :] = frames_ref[f, step * group + g].astype(F32)
            for g in range(group):
                row = step * (group // 2) + (g + 1) // 2
                for b in range(3):
                    col = tmp[g, pl.ds(7 + b, out_w, stride=2), :].astype(BF16)
                    xcols[f, row, (g + 1) % 2, :, :, b * ch : (b + 1) * ch] = col.reshape(
                        parts, cw, ch
                    )
            return carry

        lax.fori_loop(0, height // group, spread, 0)

    def row_taps(f, i0, count, *part):
        views = [
            xcols[(f, pl.ds(i0, count), 0, *part)],
            xcols[(f, pl.ds(i0, count), 1, *part)],
            xcols[(f, pl.ds(i0 + 1, count), 0, *part)],
        ]
        return jnp.concatenate([v.reshape(-1, 3 * ch) for v in views], axis=1)

    fetch[per].wait()
    pl.semaphore_wait(barrier, n - 1)

    my_q = me // q_devs
    mine = pl.ds(me * per, per)

    def send_map(h, j):
        @pl.when(j != me)
        def _():
            remote(spat.at[h, j], land.at[h, mine], send1, recv1.at[h], j).start()

        @pl.when(j == me)
        def _():
            pltpu.make_async_copy(spat.at[h, j], land.at[h, mine], recv1.at[h]).start()

    def conv(s, carry):
        q = lax.rem(my_q + 1 + s, q_count)
        devs = pl.ds(q * q_devs, q_devs)
        for f in range(per):
            out = jnp.dot(
                row_taps(f, q * q_rows, q_rows), ws_ref[...], preferred_element_type=F32
            )
            out = out.reshape(q_devs, parts, pp, ch).astype(BF16)
            for h in range(parts):
                spat[h, devs, f] = out[:, h]

        def first(k, c):
            send_map(0, q * q_devs + lax.rem(me + k, q_devs))
            return c

        lax.fori_loop(0, q_devs, first, 0)
        return carry

    lax.fori_loop(0, q_count, conv, 0)

    def later(i, carry):
        send_map(1 + i // n, lax.rem(me + 1 + lax.rem(i, n), n))
        return carry

    lax.fori_loop(0, (parts - 1) * n, later, 0)

    fetch[per + 1].wait()
    fetch[per + 2].wait()

    def clear(t, carry):
        zero = jnp.zeros((t_len, pp, ch), BF16)
        s0[pl.ds(t * t_len, t_len)] = zero
        s1[pl.ds(t * t_len, t_len)] = zero
        d1[pl.ds(length + t * t_len, t_len)] = zero
        d0[pl.ds(length + t * t_len, t_len)] = zero
        return carry

    lax.fori_loop(0, t_count, clear, 0)
    sum_s[...] = jnp.zeros_like(sum_s)
    sum_t[...] = jnp.zeros_like(sum_t)
    for layer in range(layers):
        for tap in range(taps):
            w = wt_ref[layer, tap * ch : (tap + 1) * ch, :]
            wback[layer, tap * ch : (tap + 1) * ch, :] = w.astype(F32).T.astype(BF16)

    def lagged(ref, layer, t0):
        return jnp.concatenate(
            [flat(ref[pl.ds(length + t0 - delay(layer, k), t_len)]) for k in range(taps)], axis=1
        )

    def led(ref, layer, t0):
        return jnp.concatenate(
            [flat(ref[pl.ds(t0 + delay(layer, k), t_len)]) for k in range(taps)], axis=1
        )

    def outer(x, y):
        return lax.dot_general(x, y, (((0,), (0,)), ((), ())), preferred_element_type=F32)

    def steps(count, body):
        if count == 1:
            body(0)
        else:
            lax.fori_loop(0, count, lambda t, c: (body(t), c)[1], 0)

    def temporal(h, carry):
        cols = pl.ds(pl.multiple_of(h * pp, pp), pp)
        drain(land.at[h], recv1.at[h])

        def forward(t):
            t0 = t * t_len
            state = land[h, pl.ds(t0, t_len)]
            s0[pl.ds(length + t0, t_len)] = state
            z = jnp.dot(lagged(s0, 0, t0), wt_ref[0], preferred_element_type=F32)
            act = unflat(jnp.tanh(z))
            act0[pl.ds(t0, t_len)] = act
            state = (state.astype(F32) + act).astype(BF16)
            s1[pl.ds(length + t0, t_len)] = state
            moved = lagged(s1, 1, t0)
            act = unflat(jnp.tanh(jnp.dot(moved, wt_ref[1], preferred_element_type=F32)))
            feat_ref[pl.ds(t0, t_len), cols] = (state.astype(F32) + act).astype(BF16)
            cot = cot_ref[pl.ds(t0, t_len), cols].astype(F32)
            dz = (cot * (1.0 - act * act)).astype(BF16)
            d1[pl.ds(t0, t_len)] = dz
            sum_t[tap_rows : 2 * tap_rows, :] += outer(moved, flat(dz))

        steps(t_count, forward)

        def backward(s):
            t0 = (t_count - 1 - s) * t_len
            state = cot_ref[pl.ds(t0, t_len), cols].astype(F32) + unflat(
                jnp.dot(led(d1, 1, t0), wback[1], preferred_element_type=F32)
            )
            act = act0[pl.ds(t0, t_len)]
            dz = (state * (1.0 - act * act)).astype(BF16)
            d0[pl.ds(t0, t_len)] = dz
            state = state + unflat(jnp.dot(led(d0, 0, t0), wback[0], preferred_element_type=F32))
            maps[h, pl.ds(t0, t_len)] = state.astype(BF16)
            sum_t[0:tap_rows, :] += outer(lagged(s0, 0, t0), flat(dz))

        steps(t_count, backward)

        def send(k, c):
            j = lax.rem(me + k, n)
            remote(
                maps.at[h, pl.ds(j * per, per)], back.at[h, me], send2, recv2.at[h], j
            ).start()
            return c

        lax.fori_loop(1, n, send, 0)
        pltpu.make_async_copy(maps.at[h, mine], back.at[h, me], recv2.at[h]).start()
        return carry

    lax.fori_loop(0, parts, temporal, 0)

    def conv_grad(h):
        drain(back.at[h], recv2.at[h])

        def rows(s):
            i0 = s * g_rows
            x = jnp.concatenate([row_taps(f, i0, g_rows, h) for f in range(per)], axis=0)
            g = [flat(back[h, pl.ds(s * g_devs, g_devs), f]) for f in range(per)]
            sum_s[0:sp_rows, :] += outer(x, jnp.concatenate(g, axis=0))

        steps(g_count, rows)

    store = pltpu.make_async_copy(feat_ref, feat_hbm, load.at[0])
    store.start()
    hops = [red_t.start, red_t.scatter, red_t.gather, red_t.exchange]
    hops[0]()
    for h in range(parts):
        conv_grad(h)
        if h + 1 < min(parts, len(hops)):
            hops[h + 1]()
    red_s.start()
    for hop in hops[max(1, min(parts, len(hops))) :]:
        hop()
    red_s.scatter()
    red_t.finish()
    red_s.gather()
    red_s.exchange()
    red_s.finish()

    store.wait()
    red_s.sent()
    red_t.sent()
    for ref, sem in ((land, send1), (back, send2)):
        for h in range(parts):
            drain(spat.at[h, pl.ds(0, n - 1)], sem)


def reduce_scratch(n, total_rows, ch):
    chips = n // 2
    rows = -(-total_rows // (16 * n)) * 16
    dma = pltpu.SemaphoreType.DMA
    return rows * n, [
        pltpu.VMEM((2, chips, rows, ch), BF16),
        pltpu.VMEM((chips, rows, ch), BF16),
        pltpu.VMEM((chips, rows, ch), BF16),
        pltpu.VMEM((chips, rows, ch), BF16),
        pltpu.VMEM((rows, ch), BF16),
        pltpu.VMEM((2, chips, rows, ch), BF16),
        dma((4,)),
        dma((5,)),
    ]


def local(n, frames, w_spatial, w_temporal, dilations, offsets, cotangent):
    per, height, width, ch = frames.shape
    length, pix, _ = cotangent.shape
    layers, taps = offsets.shape
    out_h, out_w = height // 2, width // 2
    sp_rows, tp_rows = 9 * ch, layers * taps * ch
    parts = PARTS if pix == out_w and pix % (16 * PARTS) == 0 else 1
    pp = pix // parts
    pad_s, red_s = reduce_scratch(n, sp_rows, ch)
    pad_t, red_t = reduce_scratch(n, tp_rows, ch)
    smem = pl.BlockSpec(memory_space=pltpu.SMEM)
    hbm = pl.BlockSpec(memory_space=pltpu.HBM)
    dma = pltpu.SemaphoreType.DMA
    features, grad_spatial, grad_temporal = pl.pallas_call(
        functools.partial(kernel, n),
        out_shape=(
            jax.ShapeDtypeStruct((length, pix, ch), BF16),
            jax.ShapeDtypeStruct((2, n // 2, pad_s // n, ch), BF16),
            jax.ShapeDtypeStruct((2, n // 2, pad_t // n, ch), BF16),
        ),
        in_specs=[smem, smem, hbm, hbm, hbm, hbm],
        out_specs=(hbm, hbm, hbm),
        scratch_shapes=[
            pltpu.VMEM(cotangent.shape, BF16),
            pltpu.VMEM(frames.shape, BF16),
            pltpu.VMEM((sp_rows, ch), BF16),
            pltpu.VMEM((layers, taps * ch, ch), BF16),
            pltpu.VMEM(cotangent.shape, BF16),
            pltpu.VMEM((8, width + 8, ch), F32),
            pltpu.VMEM((per, out_h + 1, 2, parts, out_w // parts, 3 * ch), BF16),
            pltpu.VMEM((parts, n, per, pp, ch), BF16),
            pltpu.VMEM((parts, length, pp, ch), BF16),
            pltpu.VMEM((2 * length, pp, ch), BF16),
            pltpu.VMEM((2 * length, pp, ch), BF16),
            pltpu.VMEM((length, pp, ch), F32),
            pltpu.VMEM((2 * length, pp, ch), BF16),
            pltpu.VMEM((2 * length, pp, ch), BF16),
            pltpu.VMEM((parts, length, pp, ch), BF16),
            pltpu.VMEM((parts, n, per, pp, ch), BF16),
            pltpu.VMEM((layers, taps * ch, ch), BF16),
            pltpu.VMEM((pad_s, ch), F32),
            pltpu.VMEM((pad_t, ch), F32),
            *red_s,
            *red_t,
            dma,
            dma((parts,)),
            dma,
            dma((parts,)),
            dma((per + 3,)),
        ],
        compiler_params=pltpu.CompilerParams(
            collective_id=0, has_side_effects=True, vmem_limit_bytes=60 * 1024 * 1024
        ),
        cost_estimate=pl.CostEstimate(
            flops=2 * (length * pix) * ch * ch * 36, bytes_accessed=8 << 20, transcendentals=0
        ),
    )(
        dilations,
        offsets,
        frames,
        w_spatial.reshape(sp_rows, ch),
        w_temporal.reshape(layers, taps * ch, ch),
        cotangent,
    )
    return (
        features,
        grad_spatial.reshape(-1, ch)[:sp_rows].astype(F32).reshape(3, 3, ch, ch),
        grad_temporal.reshape(-1, ch)[:tp_rows].astype(F32).reshape(layers, taps, ch, ch),
    )


def solution(mesh):
    in_specs = (
        P(("groups", "seq"), None, None, None),
        P(),
        P(),
        P(),
        P(),
        P("groups", "seq", None),
    )
    out_specs = (
        P("groups", "seq", None),
        P("groups", None, None, None),
        P("groups", None, None, None),
    )
    return jax.shard_map(
        functools.partial(local, mesh.shape["seq"]),
        mesh=mesh,
        in_specs=in_specs,
        out_specs=out_specs,
        check_vma=False,
    )
```

```python
import functools

import jax
import jax.numpy as jnp
from jax import lax
from jax.experimental import pallas as pl
from jax.experimental.pallas import tpu as pltpu
from jax.sharding import PartitionSpec as P

BF16 = jnp.bfloat16
F32 = jnp.float32
MESH = pl.DeviceIdType.MESH
PARTS = 4


def remote(src, dst, send, recv, to):
    return pltpu.make_async_remote_copy(
        src_ref=src,
        dst_ref=dst,
        send_sem=send,
        recv_sem=recv,
        device_id={"seq": to},
        device_id_type=MESH,
    )


def drain(ref, sem):
    pltpu.make_async_copy(ref, ref, sem).wait()


class Reduce:
    def __init__(self, n, out, total, pair_out, pair_in, chip_out, chip_in, own, gathered, send, recv):
        self.total, self.pair_out, self.pair_in = total, pair_out, pair_in
        self.chip_out, self.chip_in, self.own = chip_out, chip_in, own
        self.gathered, self.send, self.recv, self.out = gathered, send, recv, out
        self.chips = n // 2
        me = lax.axis_index("seq")
        self.core, self.chip = lax.rem(me, 2), me // 2
        self.partner = me + 1 - 2 * self.core
        self.rows, self.ch = own.shape
        self.half = self.chips * self.rows
        self.pair = remote(
            pair_out.at[1 - self.core], pair_in, send.at[0], recv.at[0], self.partner
        )
        self.swap = remote(
            gathered.at[self.core], gathered.at[self.core], send.at[3], recv.at[3], self.partner
        )

    def pieces(self, x):
        return x.reshape(self.chips, self.rows, self.ch)

    def chips_loop(self, src_of, dst, hop):
        def step(k, carry):
            c = lax.rem(self.chip + k, self.chips)
            remote(
                src_of(c), dst, self.send.at[hop], self.recv.at[hop], 2 * c + self.core
            ).start()
            return carry

        lax.fori_loop(1, self.chips, step, 0)

    def start(self):
        for c in range(2):
            part = self.total[c * self.half : (c + 1) * self.half, :]
            self.pair_out[c] = self.pieces(part.astype(BF16))
        self.pair.start()

    def scatter(self):
        at = pl.multiple_of(self.core * self.half, self.half)
        mine = self.pieces(self.total[pl.ds(at, self.half), :])
        self.pair.wait_recv()
        self.chip_out[...] = (mine + self.pair_in[...].astype(F32)).astype(BF16)
        dst = self.chip_in.at[self.chip]
        self.chips_loop(lambda c: self.chip_out.at[c], dst, 1)
        pltpu.make_async_copy(self.chip_out.at[self.chip], dst, self.recv.at[1]).start()

    def gather(self):
        drain(self.chip_in, self.recv.at[1])
        self.own[...] = jnp.sum(self.chip_in[...].astype(F32), axis=0).astype(BF16)
        dst = self.gathered.at[self.core, self.chip]
        self.chips_loop(lambda c: self.own, dst, 2)
        pltpu.make_async_copy(self.own, dst, self.recv.at[2]).start()

    def exchange(self):
        drain(self.gathered.at[self.core], self.recv.at[2])
        self.swap.start()
        self.widen(self.core)

    def finish(self):
        self.swap.wait_recv()
        self.widen(1 - self.core)
        self.store().start()

    def widen(self, side):
        at = pl.multiple_of(side * self.half, self.half)
        self.total[pl.ds(at, self.half), :] = (
            self.gathered[side].astype(F32).reshape(self.half, self.ch)
        )

    def store(self):
        held = self.total.at[pl.ds(0, self.out.shape[0])]
        return pltpu.make_async_copy(held, self.out, self.recv.at[4])

    def sent(self):
        self.pair.wait_send()
        self.swap.wait_send()
        most = self.chip_out.at[pl.ds(0, self.chips - 1)]
        drain(most, self.send.at[1])
        drain(most, self.send.at[2])
        self.store().wait()


def kernel(
    n,
    dil_ref,
    off_ref,
    frames_hbm,
    ws_hbm,
    wt_hbm,
    cot_hbm,
    feat_hbm,
    gs_hbm,
    gt_hbm,
    feat_ref,
    frames_ref,
    ws_ref,
    wt_ref,
    cot_ref,
    tmp,
    xcols,
    spat,
    land,
    s0,
    s1,
    act0,
    d1,
    d0,
    maps,
    back,
    wback,
    sum_s,
    sum_t,
    turned_s,
    turned_t,
    *rest,
):
    red_s = Reduce(n, gs_hbm, sum_s, *rest[0:8])
    red_t = Reduce(n, gt_hbm, sum_t, *rest[8:16])
    send1, recv1, send2, recv2, load = rest[16:]
    me = lax.axis_index("seq")
    per, height, width, ch = frames_ref.shape
    length, pix, _ = cot_ref.shape
    layers, taps = off_ref.shape
    parts, _, _, pp, _ = spat.shape
    out_h, out_w = height // 2, width // 2
    cw = out_w // parts
    q_count = 4
    q_rows = out_h // q_count
    q_devs = n // q_count
    g_count = max(1, per * out_h * cw // 512)
    g_rows, g_devs = out_h // g_count, n // g_count
    t_count = max(1, length * pp // 512)
    t_len = length // t_count
    sp_rows = ws_ref.shape[0]
    tap_rows = taps * ch

    fetch = [
        pltpu.make_async_copy(frames_hbm.at[f], frames_ref.at[f], load.at[f]) for f in range(per)
    ]
    fetch += [
        pltpu.make_async_copy(a, b, load.at[per + i])
        for i, (a, b) in enumerate([(ws_hbm, ws_ref), (wt_hbm, wt_ref), (cot_hbm, cot_ref)])
    ]
    for copy in fetch:
        copy.start()

    def flat(x):
        if pp % 16 == 0:
            return x.reshape(-1, x.shape[-1])
        return x.astype(F32).reshape(-1, x.shape[-1]).astype(BF16)

    def unflat(x):
        return x.reshape(-1, pp, ch)

    def delay(layer, tap):
        return jnp.minimum(off_ref[layer, tap] * dil_ref[layer], length)

    barrier = pltpu.get_barrier_semaphore()

    def greet(s, carry):
        pl.semaphore_signal(
            barrier, inc=1, device_id={"seq": lax.rem(me + s, n)}, device_id_type=MESH
        )
        return carry

    lax.fori_loop(1, n, greet, 0)

    group = tmp.shape[0]
    for g in range(group):
        tmp[g, 0:8, :] = jnp.zeros((8, ch), F32)
    for f in range(per):
        xcols[f, 0, 0] = jnp.zeros((parts, cw, 3 * ch), BF16)

    for f in range(per):
        fetch[f].wait()

        def spread(step, carry):
            for g in range(group):
                tmp[g, 8 : 8 + width, :] = frames_ref[f, step * group + g].astype(F32)
            for g in range(group):
                row = step * (group // 2) + (g + 1) // 2
                for b in range(3):
                    col = tmp[g, pl.ds(7 + b, out_w, stride=2), :].astype(BF16)
                    xcols[f, row, (g + 1) % 2, :, :, b * ch : (b + 1) * ch] = col.reshape(
                        parts, cw, ch
                    )
            return carry

        lax.fori_loop(0, height // group, spread, 0)

    def row_taps(f, i0, count, *part):
        views = [
            xcols[(f, pl.ds(i0, count), 0, *part)],
            xcols[(f, pl.ds(i0, count), 1, *part)],
            xcols[(f, pl.ds(i0 + 1, count), 0, *part)],
        ]
        return jnp.concatenate([v.reshape(-1, 3 * ch) for v in views], axis=1)

    fetch[per].wait()
    pl.semaphore_wait(barrier, n - 1)

    my_q = me // q_devs
    mine = pl.ds(me * per, per)

    def send_map(h, j):
        @pl.when(j != me)
        def _():
            remote(spat.at[h, j], land.at[h, mine], send1, recv1.at[h], j).start()

        @pl.when(j == me)
        def _():
            pltpu.make_async_copy(spat.at[h, j], land.at[h, mine], recv1.at[h]).start()

    def conv(s, carry):
        q = lax.rem(my_q + 1 + s, q_count)
        devs = pl.ds(q * q_devs, q_devs)
        x = jnp.concatenate([row_taps(f, q * q_rows, q_rows) for f in range(per)], axis=0)
        out = jnp.dot(x, ws_ref[...], preferred_element_type=F32)
        out = out.reshape(per, q_devs, parts, pp, ch).astype(BF16)
        for f in range(per):
            for h in range(parts):
                spat[h, devs, f] = out[f, :, h]

        def first(k, c):
            send_map(0, q * q_devs + lax.rem(me + k, q_devs))
            return c

        lax.fori_loop(0, q_devs, first, 0)
        return carry

    lax.fori_loop(0, q_count, conv, 0)

    def later(i, carry):
        send_map(1 + i // n, lax.rem(me + 1 + lax.rem(i, n), n))
        return carry

    lax.fori_loop(0, (parts - 1) * n, later, 0)

    fetch[per + 1].wait()
    fetch[per + 2].wait()

    def clear(t, carry):
        zero = jnp.zeros((t_len, pp, ch), BF16)
        s0[pl.ds(t * t_len, t_len)] = zero
        s1[pl.ds(t * t_len, t_len)] = zero
        d1[pl.ds(length + t * t_len, t_len)] = zero
        d0[pl.ds(length + t * t_len, t_len)] = zero
        return carry

    lax.fori_loop(0, t_count, clear, 0)
    turned_s[...] = jnp.zeros_like(turned_s)
    turned_t[...] = jnp.zeros_like(turned_t)
    sum_s[sp_rows:, :] = jnp.zeros((sum_s.shape[0] - sp_rows, ch), F32)
    for layer in range(layers):
        for tap in range(taps):
            w = wt_ref[layer, tap * ch : (tap + 1) * ch, :]
            wback[layer, tap * ch : (tap + 1) * ch, :] = w.astype(F32).T.astype(BF16)

    def lagged(ref, layer, t0):
        return jnp.concatenate(
            [flat(ref[pl.ds(length + t0 - delay(layer, k), t_len)]) for k in range(taps)], axis=1
        )

    def led(ref, layer, t0):
        return jnp.concatenate(
            [flat(ref[pl.ds(t0 + delay(layer, k), t_len)]) for k in range(taps)], axis=1
        )

    def outer(x, y):
        return lax.dot_general(x, y, (((0,), (0,)), ((), ())), preferred_element_type=F32)

    def steps(count, body):
        if count == 1:
            body(0)
        else:
            lax.fori_loop(0, count, lambda t, c: (body(t), c)[1], 0)

    def temporal(h, carry):
        cols = pl.ds(pl.multiple_of(h * pp, pp), pp)
        drain(land.at[h], recv1.at[h])

        def forward(t):
            t0 = t * t_len
            state = land[h, pl.ds(t0, t_len)]
            s0[pl.ds(length + t0, t_len)] = state
            z = jnp.dot(lagged(s0, 0, t0), wt_ref[0], preferred_element_type=F32)
            act = unflat(jnp.tanh(z))
            act0[pl.ds(t0, t_len)] = act
            state = (state.astype(F32) + act).astype(BF16)
            s1[pl.ds(length + t0, t_len)] = state
            moved = lagged(s1, 1, t0)
            act = unflat(jnp.tanh(jnp.dot(moved, wt_ref[1], preferred_element_type=F32)))
            feat_ref[pl.ds(t0, t_len), cols] = (state.astype(F32) + act).astype(BF16)
            cot = cot_ref[pl.ds(t0, t_len), cols].astype(F32)
            dz = (cot * (1.0 - act * act)).astype(BF16)
            d1[pl.ds(t0, t_len)] = dz
            turned_t[1] += outer(flat(dz), moved)

        steps(t_count, forward)

        def backward(s):
            t0 = (t_count - 1 - s) * t_len
            state = cot_ref[pl.ds(t0, t_len), cols].astype(F32) + unflat(
                jnp.dot(led(d1, 1, t0), wback[1], preferred_element_type=F32)
            )
            act = act0[pl.ds(t0, t_len)]
            dz = (state * (1.0 - act * act)).astype(BF16)
            d0[pl.ds(t0, t_len)] = dz
            state = state + unflat(jnp.dot(led(d0, 0, t0), wback[0], preferred_element_type=F32))
            maps[h, pl.ds(t0, t_len)] = state.astype(BF16)
            turned_t[0] += outer(flat(dz), lagged(s0, 0, t0))

        steps(t_count, backward)

        def send(k, c):
            j = lax.rem(me + k, n)
            remote(
                maps.at[h, pl.ds(j * per, per)], back.at[h, me], send2, recv2.at[h], j
            ).start()
            return c

        lax.fori_loop(1, n, send, 0)
        pltpu.make_async_copy(maps.at[h, mine], back.at[h, me], recv2.at[h]).start()
        return carry

    lax.fori_loop(0, parts, temporal, 0)

    def conv_grad(h):
        drain(back.at[h], recv2.at[h])

        def rows(s):
            i0 = s * g_rows
            x = jnp.concatenate([row_taps(f, i0, g_rows, h) for f in range(per)], axis=0)
            g = [flat(back[h, pl.ds(s * g_devs, g_devs), f]) for f in range(per)]
            turned_s[...] += outer(jnp.concatenate(g, axis=0), x)

        steps(g_count, rows)

    store = pltpu.make_async_copy(feat_ref, feat_hbm, load.at[0])
    store.start()
    for layer in range(layers):
        for k in range(taps):
            at = layer * tap_rows + k * ch
            sum_t[at : at + ch, :] = turned_t[layer, :, k * ch : (k + 1) * ch].T
    hops = [red_t.start, red_t.scatter, red_t.gather, red_t.exchange]
    hops[0]()
    for h in range(parts):
        conv_grad(h)
        if h + 1 < min(parts, len(hops)):
            hops[h + 1]()
    for at in range(0, sp_rows, ch):
        sum_s[at : at + ch, :] = turned_s[:, at : at + ch].T
    red_s.start()
    for hop in hops[max(1, min(parts, len(hops))) :]:
        hop()
    red_s.scatter()
    red_t.finish()
    red_s.gather()
    red_s.exchange()
    red_s.finish()

    store.wait()
    red_s.sent()
    red_t.sent()
    for ref, sem in ((land, send1), (back, send2)):
        for h in range(parts):
            drain(spat.at[h, pl.ds(0, n - 1)], sem)


def reduce_scratch(n, total_rows, ch):
    chips = n // 2
    rows = -(-total_rows // (16 * n)) * 16
    dma = pltpu.SemaphoreType.DMA
    return rows * n, [
        pltpu.VMEM((2, chips, rows, ch), BF16),
        pltpu.VMEM((chips, rows, ch), BF16),
        pltpu.VMEM((chips, rows, ch), BF16),
        pltpu.VMEM((chips, rows, ch), BF16),
        pltpu.VMEM((rows, ch), BF16),
        pltpu.VMEM((2, chips, rows, ch), BF16),
        dma((4,)),
        dma((5,)),
    ]


def hand_over(*arrays):
    count = len(arrays)

    def body(*refs):
        sems = refs[2 * count]
        copies = [
            pltpu.make_async_copy(refs[i], refs[count + i], sems.at[i]) for i in range(count)
        ]
        for copy in copies:
            copy.start()
        for copy in copies:
            copy.wait()

    hbm = pl.BlockSpec(memory_space=pltpu.HBM)
    return pl.pallas_call(
        body,
        out_shape=tuple(jax.ShapeDtypeStruct(a.shape, a.dtype) for a in arrays),
        in_specs=[hbm] * count,
        out_specs=(hbm,) * count,
        scratch_shapes=[pltpu.SemaphoreType.DMA((count,))],
        compiler_params=pltpu.CompilerParams(vmem_limit_bytes=60 * 1024 * 1024),
    )(*arrays)


def local(n, frames, w_spatial, w_temporal, dilations, offsets, cotangent):
    per, height, width, ch = frames.shape
    length, pix, _ = cotangent.shape
    layers, taps = offsets.shape
    out_h, out_w = height // 2, width // 2
    sp_rows, tp_rows = 9 * ch, layers * taps * ch
    parts = PARTS if pix == out_w and pix % (16 * PARTS) == 0 else 1
    pp = pix // parts
    pad_s, red_s = reduce_scratch(n, sp_rows, ch)
    pad_t, red_t = reduce_scratch(n, tp_rows, ch)
    smem = pl.BlockSpec(memory_space=pltpu.SMEM)
    hbm = pl.BlockSpec(memory_space=pltpu.HBM)
    dma = pltpu.SemaphoreType.DMA
    features, grad_spatial, grad_temporal = pl.pallas_call(
        functools.partial(kernel, n),
        out_shape=(
            jax.ShapeDtypeStruct((length, pix, ch), BF16),
            jax.ShapeDtypeStruct((sp_rows, ch), F32),
            jax.ShapeDtypeStruct((tp_rows, ch), F32),
        ),
        in_specs=[smem, smem, hbm, hbm, hbm, hbm],
        out_specs=(hbm, hbm, hbm),
        scratch_shapes=[
            pltpu.VMEM(cotangent.shape, BF16),
            pltpu.VMEM(frames.shape, BF16),
            pltpu.VMEM((sp_rows, ch), BF16),
            pltpu.VMEM((layers, taps * ch, ch), BF16),
            pltpu.VMEM(cotangent.shape, BF16),
            pltpu.VMEM((8, width + 8, ch), F32),
            pltpu.VMEM((per, out_h + 1, 2, parts, out_w // parts, 3 * ch), BF16),
            pltpu.VMEM((parts, n, per, pp, ch), BF16),
            pltpu.VMEM((parts, length, pp, ch), BF16),
            pltpu.VMEM((2 * length, pp, ch), BF16),
            pltpu.VMEM((2 * length, pp, ch), BF16),
            pltpu.VMEM((length, pp, ch), F32),
            pltpu.VMEM((2 * length, pp, ch), BF16),
            pltpu.VMEM((2 * length, pp, ch), BF16),
            pltpu.VMEM((parts, length, pp, ch), BF16),
            pltpu.VMEM((parts, n, per, pp, ch), BF16),
            pltpu.VMEM((layers, taps * ch, ch), BF16),
            pltpu.VMEM((pad_s, ch), F32),
            pltpu.VMEM((pad_t, ch), F32),
            pltpu.VMEM((ch, sp_rows), F32),
            pltpu.VMEM((layers, ch, taps * ch), F32),
            *red_s,
            *red_t,
            dma,
            dma((parts,)),
            dma,
            dma((parts,)),
            dma((per + 3,)),
        ],
        compiler_params=pltpu.CompilerParams(
            collective_id=0, has_side_effects=True, vmem_limit_bytes=60 * 1024 * 1024
        ),
        cost_estimate=pl.CostEstimate(
            flops=2 * (length * pix) * ch * ch * 36, bytes_accessed=8 << 20, transcendentals=0
        ),
    )(
        dilations,
        offsets,
        frames,
        w_spatial.reshape(sp_rows, ch),
        w_temporal.reshape(layers, taps * ch, ch),
        cotangent,
    )
    features, grad_spatial, grad_temporal = hand_over(features, grad_spatial, grad_temporal)
    return (
        features,
        grad_spatial.reshape(3, 3, ch, ch),
        grad_temporal.reshape(layers, taps, ch, ch),
    )


def solution(mesh):
    in_specs = (
        P(("groups", "seq"), None, None, None),
        P(),
        P(),
        P(),
        P(),
        P("groups", "seq", None),
    )
    out_specs = (
        P("groups", "seq", None),
        P("groups", None, None, None),
        P("groups", None, None, None),
    )
    return jax.shard_map(
        functools.partial(local, mesh.shape["seq"]),
        mesh=mesh,
        in_specs=in_specs,
        out_specs=out_specs,
        check_vma=False,
    )
```

```python
import functools

import jax
import jax.numpy as jnp
from jax import lax
from jax.experimental import pallas as pl
from jax.experimental.pallas import tpu as pltpu
from jax.sharding import PartitionSpec as P

BF16 = jnp.bfloat16
F32 = jnp.float32
MESH = pl.DeviceIdType.MESH
PARTS = 4
NEAR_S = 2
NEAR_T = 4


def remote(src, dst, send, recv, to):
    return pltpu.make_async_remote_copy(
        src_ref=src,
        dst_ref=dst,
        send_sem=send,
        recv_sem=recv,
        device_id={"seq": to},
        device_id_type=MESH,
    )


def drain(ref, sem):
    pltpu.make_async_copy(ref, ref, sem).wait()


class Reduce:
    def __init__(self, n, size, out, total, near_out, near_in, far_out, far_in, own, gathered, *sems):
        self.out, self.total, self.near_out, self.near_in = out, total, near_out, near_in
        self.far_out, self.far_in, self.own, self.gathered = far_out, far_in, own, gathered
        self.send, self.recv = sems
        self.size, self.groups = size, n // size
        me = lax.axis_index("seq")
        self.near, self.far = lax.rem(me, size), me // size
        self.rows, self.ch = own.shape
        self.slab = self.groups * self.rows

    def near_loop(self, src_of, dst, hop):
        for k in range(1, self.size):
            c = lax.rem(self.near + k, self.size)
            to = self.far * self.size + c
            remote(src_of(c), dst, self.send.at[hop], self.recv.at[hop], to).start()

    def far_loop(self, src_of, dst, hop):
        def step(k, carry):
            g = lax.rem(self.far + k, self.groups)
            to = g * self.size + self.near
            remote(src_of(g), dst, self.send.at[hop], self.recv.at[hop], to).start()
            return carry

        lax.fori_loop(1, self.groups, step, 0)

    def span(self, c):
        return pl.ds(pl.multiple_of(c * self.slab, self.slab), self.slab)

    def pieces(self, x):
        return x.reshape(self.groups, self.rows, self.ch)

    def start(self):
        for c in range(self.size):
            part = self.total[c * self.slab : (c + 1) * self.slab, :]
            self.near_out[c] = self.pieces(part.astype(BF16))
        self.near_loop(lambda c: self.near_out.at[c], self.near_in.at[self.near], 0)

    def scatter(self):
        mine = self.pieces(self.total[self.span(self.near), :])
        drain(self.near_in.at[pl.ds(0, self.size - 1)], self.recv.at[0])
        for k in range(1, self.size):
            mine = mine + self.near_in[lax.rem(self.near + k, self.size)].astype(F32)
        self.far_out[...] = mine.astype(BF16)
        dst = self.far_in.at[self.far]
        self.far_loop(lambda g: self.far_out.at[g], dst, 1)
        pltpu.make_async_copy(self.far_out.at[self.far], dst, self.recv.at[1]).start()

    def gather(self):
        drain(self.far_in, self.recv.at[1])
        self.own[...] = jnp.sum(self.far_in[...].astype(F32), axis=0).astype(BF16)
        dst = self.gathered.at[self.near, self.far]
        self.far_loop(lambda g: self.own, dst, 2)
        pltpu.make_async_copy(self.own, dst, self.recv.at[2]).start()

    def exchange(self):
        mine = self.gathered.at[self.near]
        drain(mine, self.recv.at[2])
        self.near_loop(lambda c: mine, mine, 3)
        self.widen(self.near)

    def finish(self):
        drain(self.near_in.at[pl.ds(0, self.size - 1)], self.recv.at[3])
        for k in range(1, self.size):
            self.widen(lax.rem(self.near + k, self.size))
        self.store().start()

    def widen(self, c):
        self.total[self.span(c), :] = self.gathered[c].astype(F32).reshape(self.slab, self.ch)

    def store(self):
        held = self.total.at[pl.ds(0, self.out.shape[0])]
        return pltpu.make_async_copy(held, self.out, self.recv.at[4])

    def sent(self):
        for hop in (0, 3):
            drain(self.near_in.at[pl.ds(0, self.size - 1)], self.send.at[hop])
        for hop in (1, 2):
            drain(self.far_out.at[pl.ds(0, self.groups - 1)], self.send.at[hop])
        self.store().wait()


def kernel(
    n,
    dil_ref,
    off_ref,
    frames_hbm,
    ws_hbm,
    wt_hbm,
    cot_hbm,
    feat_hbm,
    gs_hbm,
    gt_hbm,
    feat_ref,
    frames_ref,
    ws_ref,
    wt_ref,
    cot_ref,
    tmp,
    xcols,
    spat,
    land,
    s0,
    s1,
    act0,
    d1,
    d0,
    maps,
    back,
    wback,
    sum_s,
    sum_t,
    turned_s,
    turned_t,
    *rest,
):
    red_s = Reduce(n, NEAR_S, gs_hbm, sum_s, *rest[0:8])
    red_t = Reduce(n, NEAR_T, gt_hbm, sum_t, *rest[8:16])
    send1, recv1, send2, recv2, load = rest[16:]
    me = lax.axis_index("seq")
    per, height, width, ch = frames_hbm.shape
    length, pix, _ = cot_ref.shape
    layers, taps = off_ref.shape
    parts, _, _, pp, _ = spat.shape
    out_h, out_w = height // 2, width // 2
    cw = out_w // parts
    q_count = 4
    q_rows = out_h // q_count
    q_devs = n // q_count
    g_count = max(1, per * out_h * cw // 512)
    g_rows, g_devs = out_h // g_count, n // g_count
    t_count = max(1, length * pp // 512)
    t_len = length // t_count
    sp_rows = ws_ref.shape[0]
    tap_rows = taps * ch

    my_q = me // q_devs
    q_in = height // q_count

    for s in range(q_count):
        q = lax.rem(my_q + 1 + s, q_count)
        above = jnp.maximum(q * q_in - 1, 0)
        for f in range(per):
            pltpu.make_async_copy(
                frames_hbm.at[f, pl.ds(q * q_in, q_in)],
                frames_ref.at[q, f, pl.ds(1, q_in)],
                load.at[q],
            ).start()
            pltpu.make_async_copy(
                frames_hbm.at[f, pl.ds(above, 1)], frames_ref.at[q, f, pl.ds(0, 1)], load.at[q]
            ).start()
    fetch = [
        pltpu.make_async_copy(a, b, load.at[q_count + i])
        for i, (a, b) in enumerate([(ws_hbm, ws_ref), (wt_hbm, wt_ref), (cot_hbm, cot_ref)])
    ]
    for copy in fetch:
        copy.start()

    def flat(x):
        if pp % 16 == 0:
            return x.reshape(-1, x.shape[-1])
        return x.astype(F32).reshape(-1, x.shape[-1]).astype(BF16)

    def unflat(x):
        return x.reshape(-1, pp, ch)

    def delay(layer, tap):
        return jnp.minimum(off_ref[layer, tap] * dil_ref[layer], length)

    barrier = pltpu.get_barrier_semaphore()

    def greet(s, carry):
        pl.semaphore_signal(
            barrier, inc=1, device_id={"seq": lax.rem(me + s, n)}, device_id_type=MESH
        )
        return carry

    lax.fori_loop(1, n, greet, 0)

    for f in range(per):
        for g in range(q_in + 1):
            tmp[f, g, 0:8, :] = jnp.zeros((8, ch), F32)

    def spread(q):
        drain(frames_ref.at[q], load.at[q])
        for f in range(per):
            for g in range(q_in + 1):
                row = frames_ref[q, f, g].astype(F32)
                if g == 0:
                    row = jnp.where(q > 0, row, 0.0)
                tmp[f, g, 8 : 8 + width, :] = row
            for g in range(q_in + 1):
                for b in range(3):
                    col = tmp[f, g, pl.ds(7 + b, out_w, stride=2), :].astype(BF16)
                    xcols[f, q * q_rows + g // 2, g % 2, :, :, b * ch : (b + 1) * ch] = (
                        col.reshape(parts, cw, ch)
                    )

    def row_taps(f, i0, count, *part):
        views = [
            xcols[(f, pl.ds(i0, count), 0, *part)],
            xcols[(f, pl.ds(i0, count), 1, *part)],
            xcols[(f, pl.ds(i0 + 1, count), 0, *part)],
        ]
        return jnp.concatenate([v.reshape(-1, 3 * ch) for v in views], axis=1)

    early = max(1, parts // 2)
    mine = pl.ds(me * per, per)

    def send_map(h, j):
        @pl.when(j != me)
        def _():
            remote(spat.at[h, j], land.at[h, mine], send1, recv1.at[h], j).start()

        @pl.when(j == me)
        def _():
            pltpu.make_async_copy(spat.at[h, j], land.at[h, mine], recv1.at[h]).start()

    def conv(s, carry):
        q = lax.rem(my_q + 1 + s, q_count)
        devs = pl.ds(q * q_devs, q_devs)
        spread(q)

        @pl.when(s == 0)
        def _():
            fetch[0].wait()

        x = jnp.concatenate([row_taps(f, q * q_rows, q_rows) for f in range(per)], axis=0)
        out = jnp.dot(x, ws_ref[...], preferred_element_type=F32)
        out = out.reshape(per, q_devs, parts, pp, ch).astype(BF16)
        for f in range(per):
            for h in range(parts):
                spat[h, devs, f] = out[f, :, h]

        @pl.when(s == 0)
        def _():
            pl.semaphore_wait(barrier, n - 1)

        def first(k, c):
            for h in range(early):
                send_map(h, q * q_devs + lax.rem(me + k, q_devs))
            return c

        lax.fori_loop(0, q_devs, first, 0)
        return carry

    lax.fori_loop(0, q_count, conv, 0)

    def later(i, carry):
        send_map(early + i // n, lax.rem(me + 1 + lax.rem(i, n), n))
        return carry

    lax.fori_loop(0, (parts - early) * n, later, 0)

    fetch[1].wait()
    fetch[2].wait()

    def clear(t, carry):
        zero = jnp.zeros((t_len, pp, ch), BF16)
        s0[pl.ds(t * t_len, t_len)] = zero
        s1[pl.ds(t * t_len, t_len)] = zero
        d1[pl.ds(length + t * t_len, t_len)] = zero
        d0[pl.ds(length + t * t_len, t_len)] = zero
        return carry

    lax.fori_loop(0, t_count, clear, 0)
    turned_s[...] = jnp.zeros_like(turned_s)
    turned_t[...] = jnp.zeros_like(turned_t)
    sum_s[sp_rows:, :] = jnp.zeros((sum_s.shape[0] - sp_rows, ch), F32)
    for layer in range(layers):
        for tap in range(taps):
            w = wt_ref[layer, tap * ch : (tap + 1) * ch, :]
            wback[layer, tap * ch : (tap + 1) * ch, :] = w.astype(F32).T.astype(BF16)

    def lagged(ref, layer, t0):
        return jnp.concatenate(
            [flat(ref[pl.ds(length + t0 - delay(layer, k), t_len)]) for k in range(taps)], axis=1
        )

    def led(ref, layer, t0):
        return jnp.concatenate(
            [flat(ref[pl.ds(t0 + delay(layer, k), t_len)]) for k in range(taps)], axis=1
        )

    def outer(x, y):
        return lax.dot_general(x, y, (((0,), (0,)), ((), ())), preferred_element_type=F32)

    def steps(count, body):
        if count == 1:
            body(0)
        else:
            lax.fori_loop(0, count, lambda t, c: (body(t), c)[1], 0)

    def temporal(h, carry):
        cols = pl.ds(pl.multiple_of(h * pp, pp), pp)
        drain(land.at[h], recv1.at[h])

        def forward(t):
            t0 = t * t_len
            state = land[h, pl.ds(t0, t_len)]
            s0[pl.ds(length + t0, t_len)] = state
            z = jnp.dot(lagged(s0, 0, t0), wt_ref[0], preferred_element_type=F32)
            act = unflat(jnp.tanh(z))
            act0[pl.ds(t0, t_len)] = act
            state = (state.astype(F32) + act).astype(BF16)
            s1[pl.ds(length + t0, t_len)] = state
            moved = lagged(s1, 1, t0)
            act = unflat(jnp.tanh(jnp.dot(moved, wt_ref[1], preferred_element_type=F32)))
            feat_ref[pl.ds(t0, t_len), cols] = (state.astype(F32) + act).astype(BF16)
            cot = cot_ref[pl.ds(t0, t_len), cols].astype(F32)
            dz = (cot * (1.0 - act * act)).astype(BF16)
            d1[pl.ds(t0, t_len)] = dz
            turned_t[1] += outer(flat(dz), moved)

        steps(t_count, forward)

        def backward(s):
            t0 = (t_count - 1 - s) * t_len
            state = cot_ref[pl.ds(t0, t_len), cols].astype(F32) + unflat(
                jnp.dot(led(d1, 1, t0), wback[1], preferred_element_type=F32)
            )
            act = act0[pl.ds(t0, t_len)]
            dz = (state * (1.0 - act * act)).astype(BF16)
            d0[pl.ds(t0, t_len)] = dz
            state = state + unflat(jnp.dot(led(d0, 0, t0), wback[0], preferred_element_type=F32))
            maps[h, pl.ds(t0, t_len)] = state.astype(BF16)
            turned_t[0] += outer(flat(dz), lagged(s0, 0, t0))

        steps(t_count, backward)

        def send(k, c):
            j = lax.rem(me + k, n)
            remote(
                maps.at[h, pl.ds(j * per, per)], back.at[h, me], send2, recv2.at[h], j
            ).start()
            return c

        lax.fori_loop(1, n, send, 0)
        pltpu.make_async_copy(maps.at[h, mine], back.at[h, me], recv2.at[h]).start()
        return carry

    lax.fori_loop(0, parts, temporal, 0)

    def conv_grad(h):
        drain(back.at[h], recv2.at[h])

        def rows(s):
            i0 = s * g_rows
            x = jnp.concatenate([row_taps(f, i0, g_rows, h) for f in range(per)], axis=0)
            g = [flat(back[h, pl.ds(s * g_devs, g_devs), f]) for f in range(per)]
            turned_s[...] += outer(jnp.concatenate(g, axis=0), x)

        steps(g_count, rows)

    store = pltpu.make_async_copy(feat_ref, feat_hbm, load.at[0])
    store.start()
    for layer in range(layers):
        for k in range(taps):
            at = layer * tap_rows + k * ch
            sum_t[at : at + ch, :] = turned_t[layer, :, k * ch : (k + 1) * ch].T
    hops = [red_t.start, red_t.scatter, red_t.gather, red_t.exchange]
    hops[0]()
    for h in range(parts):
        conv_grad(h)
        if h + 1 < min(parts, len(hops)):
            hops[h + 1]()
    for at in range(0, sp_rows, ch):
        sum_s[at : at + ch, :] = turned_s[:, at : at + ch].T
    red_s.start()
    for hop in hops[max(1, min(parts, len(hops))) :]:
        hop()
    red_s.scatter()
    red_t.finish()
    red_s.gather()
    red_s.exchange()
    red_s.finish()

    store.wait()
    red_s.sent()
    red_t.sent()
    for ref, sem in ((land, send1), (back, send2)):
        for h in range(parts):
            drain(spat.at[h, pl.ds(0, n - 1)], sem)


def reduce_scratch(n, size, total_rows, ch):
    groups = n // size
    rows = -(-total_rows // (16 * n)) * 16
    dma = pltpu.SemaphoreType.DMA
    return rows * n, [
        pltpu.VMEM((size, groups, rows, ch), BF16),
        pltpu.VMEM((size, groups, rows, ch), BF16),
        pltpu.VMEM((groups, rows, ch), BF16),
        pltpu.VMEM((groups, rows, ch), BF16),
        pltpu.VMEM((rows, ch), BF16),
        pltpu.VMEM((size, groups, rows, ch), BF16),
        dma((4,)),
        dma((5,)),
    ]


def local(n, frames, w_spatial, w_temporal, dilations, offsets, cotangent):
    per, height, width, ch = frames.shape
    length, pix, _ = cotangent.shape
    layers, taps = offsets.shape
    out_h, out_w = height // 2, width // 2
    sp_rows, tp_rows = 9 * ch, layers * taps * ch
    parts = PARTS if pix == out_w and pix % (16 * PARTS) == 0 else 1
    pp = pix // parts
    pad_s, red_s = reduce_scratch(n, NEAR_S, sp_rows, ch)
    pad_t, red_t = reduce_scratch(n, NEAR_T, tp_rows, ch)
    smem = pl.BlockSpec(memory_space=pltpu.SMEM)
    hbm = pl.BlockSpec(memory_space=pltpu.HBM)
    dma = pltpu.SemaphoreType.DMA
    features, grad_spatial, grad_temporal = pl.pallas_call(
        functools.partial(kernel, n),
        out_shape=(
            jax.ShapeDtypeStruct((length, pix, ch), BF16),
            jax.ShapeDtypeStruct((sp_rows, ch), F32),
            jax.ShapeDtypeStruct((tp_rows, ch), F32),
        ),
        in_specs=[smem, smem, hbm, hbm, hbm, hbm],
        out_specs=(hbm, hbm, hbm),
        scratch_shapes=[
            pltpu.VMEM(cotangent.shape, BF16),
            pltpu.VMEM((4, per, height // 4 + 1, width, ch), BF16),
            pltpu.VMEM((sp_rows, ch), BF16),
            pltpu.VMEM((layers, taps * ch, ch), BF16),
            pltpu.VMEM(cotangent.shape, BF16),
            pltpu.VMEM((per, height // 4 + 1, width + 8, ch), F32),
            pltpu.VMEM((per, out_h + 1, 2, parts, out_w // parts, 3 * ch), BF16),
            pltpu.VMEM((parts, n, per, pp, ch), BF16),
            pltpu.VMEM((parts, length, pp, ch), BF16),
            pltpu.VMEM((2 * length, pp, ch), BF16),
            pltpu.VMEM((2 * length, pp, ch), BF16),
            pltpu.VMEM((length, pp, ch), F32),
            pltpu.VMEM((2 * length, pp, ch), BF16),
            pltpu.VMEM((2 * length, pp, ch), BF16),
            pltpu.VMEM((parts, length, pp, ch), BF16),
            pltpu.VMEM((parts, n, per, pp, ch), BF16),
            pltpu.VMEM((layers, taps * ch, ch), BF16),
            pltpu.VMEM((pad_s, ch), F32),
            pltpu.VMEM((pad_t, ch), F32),
            pltpu.VMEM((ch, sp_rows), F32),
            pltpu.VMEM((layers, ch, taps * ch), F32),
            *red_s,
            *red_t,
            dma,
            dma((parts,)),
            dma,
            dma((parts,)),
            dma((4 + 3,)),
        ],
        compiler_params=pltpu.CompilerParams(
            collective_id=0, has_side_effects=True, vmem_limit_bytes=60 * 1024 * 1024
        ),
        cost_estimate=pl.CostEstimate(
            flops=2 * (length * pix) * ch * ch * 36, bytes_accessed=8 << 20, transcendentals=0
        ),
    )(
        dilations,
        offsets,
        frames,
        w_spatial.reshape(sp_rows, ch),
        w_temporal.reshape(layers, taps * ch, ch),
        cotangent,
    )
    return (
        features,
        grad_spatial.reshape(3, 3, ch, ch),
        grad_temporal.reshape(layers, taps, ch, ch),
    )


def solution(mesh):
    in_specs = (
        P(("groups", "seq"), None, None, None),
        P(),
        P(),
        P(),
        P(),
        P("groups", "seq", None),
    )
    out_specs = (
        P("groups", "seq", None),
        P("groups", None, None, None),
        P("groups", None, None, None),
    )
    return jax.shard_map(
        functools.partial(local, mesh.shape["seq"]),
        mesh=mesh,
        in_specs=in_specs,
        out_specs=out_specs,
        check_vma=False,
    )
```

```python
import functools

import jax
import jax.numpy as jnp
from jax import lax
from jax.experimental import pallas as pl
from jax.experimental.pallas import tpu as pltpu
from jax.sharding import PartitionSpec as P

BF16 = jnp.bfloat16
F32 = jnp.float32
MESH = pl.DeviceIdType.MESH
PARTS = 2
NEAR_S = 2
NEAR_T = 4


def wrap(x, n):
    return jnp.where(x >= n, x - n, x)


def each(first, end, body):
    if end - first <= 16:
        for k in range(first, end):
            body(k)
    else:
        lax.fori_loop(first, end, lambda k, c: (body(k), c)[1], 0)


def remote(src, dst, send, recv, to):
    return pltpu.make_async_remote_copy(
        src_ref=src,
        dst_ref=dst,
        send_sem=send,
        recv_sem=recv,
        device_id={"seq": to},
        device_id_type=MESH,
    )


def drain(ref, sem):
    pltpu.make_async_copy(ref, ref, sem).wait()


class Reduce:
    def __init__(self, n, size, out, total, near_out, near_in, far_out, far_in, own, gathered, *sems):
        self.out, self.total, self.near_out, self.near_in = out, total, near_out, near_in
        self.far_out, self.far_in, self.own, self.gathered = far_out, far_in, own, gathered
        self.send, self.recv = sems
        self.size, self.groups = size, n // size
        me = lax.axis_index("seq")
        self.near, self.far = lax.rem(me, size), me // size
        self.rows, self.ch = own.shape
        self.slab = self.groups * self.rows

    def near_loop(self, src_of, dst, hop):
        for k in range(1, self.size):
            c = wrap(self.near + k, self.size)
            to = self.far * self.size + c
            remote(src_of(c), dst, self.send.at[hop], self.recv.at[hop], to).start()

    def far_loop(self, src_of, dst, hop):
        def step(k):
            g = wrap(self.far + k, self.groups)
            to = g * self.size + self.near
            remote(src_of(g), dst, self.send.at[hop], self.recv.at[hop], to).start()

        each(1, self.groups, step)

    def span(self, c):
        return pl.ds(pl.multiple_of(c * self.slab, self.slab), self.slab)

    def pieces(self, x):
        return x.reshape(self.groups, self.rows, self.ch)

    def start(self):
        for c in range(self.size):
            part = self.total[c * self.slab : (c + 1) * self.slab, :]
            self.near_out[c] = self.pieces(part.astype(BF16))
        self.near_loop(lambda c: self.near_out.at[c], self.near_in.at[self.near], 0)

    def scatter(self):
        mine = self.pieces(self.total[self.span(self.near), :])
        drain(self.near_in.at[pl.ds(0, self.size - 1)], self.recv.at[0])
        for k in range(1, self.size):
            mine = mine + self.near_in[wrap(self.near + k, self.size)].astype(F32)
        self.far_out[...] = mine.astype(BF16)
        dst = self.far_in.at[self.far]
        self.far_loop(lambda g: self.far_out.at[g], dst, 1)
        pltpu.make_async_copy(self.far_out.at[self.far], dst, self.recv.at[1]).start()

    def gather(self):
        drain(self.far_in, self.recv.at[1])
        self.own[...] = jnp.sum(self.far_in[...].astype(F32), axis=0).astype(BF16)
        dst = self.gathered.at[self.near, self.far]
        self.far_loop(lambda g: self.own, dst, 2)
        pltpu.make_async_copy(self.own, dst, self.recv.at[2]).start()

    def exchange(self):
        mine = self.gathered.at[self.near]
        drain(mine, self.recv.at[2])
        self.near_loop(lambda c: mine, mine, 3)
        self.store(self.near)

    def finish(self):
        drain(self.near_in.at[pl.ds(0, self.size - 1)], self.recv.at[3])
        for k in range(1, self.size):
            self.store(wrap(self.near + k, self.size))

    def store(self, c):
        pltpu.make_async_copy(self.gathered.at[c], self.out.at[c], self.recv.at[4]).start()

    def sent(self):
        for hop in (0, 3):
            drain(self.near_in.at[pl.ds(0, self.size - 1)], self.send.at[hop])
        for hop in (1, 2):
            drain(self.far_out.at[pl.ds(0, self.groups - 1)], self.send.at[hop])
        drain(self.gathered, self.recv.at[4])


def kernel(
    n,
    dil_ref,
    off_ref,
    frames_hbm,
    ws_hbm,
    wt_hbm,
    cot_hbm,
    feat_hbm,
    gs_hbm,
    gt_hbm,
    feat_ref,
    frames_ref,
    ws_ref,
    wt_ref,
    cot_ref,
    tmp,
    xcols,
    spat,
    land,
    s0,
    s1,
    act0,
    d1,
    d0,
    maps,
    back,
    wback,
    sum_s,
    sum_t,
    turned_s,
    turned_t,
    *rest,
):
    red_s = Reduce(n, NEAR_S, gs_hbm, sum_s, *rest[0:8])
    red_t = Reduce(n, NEAR_T, gt_hbm, sum_t, *rest[8:16])
    send1, recv1, send2, recv2, load = rest[16:]
    me = lax.axis_index("seq")
    per, height, width, ch = frames_hbm.shape
    length, pix, _ = cot_ref.shape
    layers, taps = off_ref.shape
    parts, _, _, pp, _ = spat.shape
    out_h, out_w = height // 2, width // 2
    cw = out_w // parts
    q_count = 4
    q_rows = out_h // q_count
    q_devs = n // q_count
    g_count = max(1, per * out_h * cw // 512)
    g_rows, g_devs = out_h // g_count, n // g_count
    t_count = max(1, length * pp // 512)
    t_len = length // t_count
    sp_rows = ws_ref.shape[0]
    tap_rows = taps * ch

    my_q = me // q_devs
    q_in = height // q_count

    for s in range(q_count):
        q = lax.rem(my_q + 1 + s, q_count)
        above = jnp.maximum(q * q_in - 1, 0)
        for f in range(per):
            pltpu.make_async_copy(
                frames_hbm.at[f, pl.ds(q * q_in, q_in)],
                frames_ref.at[q, f, pl.ds(1, q_in)],
                load.at[q],
            ).start()
            pltpu.make_async_copy(
                frames_hbm.at[f, pl.ds(above, 1)], frames_ref.at[q, f, pl.ds(0, 1)], load.at[q]
            ).start()
    fetch = [
        pltpu.make_async_copy(a, b, load.at[q_count + i])
        for i, (a, b) in enumerate([(ws_hbm, ws_ref), (wt_hbm, wt_ref), (cot_hbm, cot_ref)])
    ]
    for copy in fetch:
        copy.start()

    def flat(x):
        if pp % 16 == 0:
            return x.reshape(-1, x.shape[-1])
        return x.astype(F32).reshape(-1, x.shape[-1]).astype(BF16)

    def unflat(x):
        return x.reshape(-1, pp, ch)

    def delay(layer, tap):
        return jnp.minimum(off_ref[layer, tap] * dil_ref[layer], length)

    barrier = pltpu.get_barrier_semaphore()

    def greet(s):
        pl.semaphore_signal(
            barrier, inc=1, device_id={"seq": wrap(me + s, n)}, device_id_type=MESH
        )

    each(1, n, greet)

    for f in range(per):
        for g in range(q_in + 1):
            tmp[f, g, 0:8, :] = jnp.zeros((8, ch), F32)

    def spread(q):
        drain(frames_ref.at[q], load.at[q])
        for f in range(per):
            for g in range(q_in + 1):
                row = frames_ref[q, f, g].astype(F32)
                if g == 0:
                    row = jnp.where(q > 0, row, 0.0)
                tmp[f, g, 8 : 8 + width, :] = row
            for g in range(q_in + 1):
                for b in range(3):
                    col = tmp[f, g, pl.ds(7 + b, out_w, stride=2), :].astype(BF16)
                    xcols[f, q * q_rows + g // 2, g % 2, :, :, b * ch : (b + 1) * ch] = (
                        col.reshape(parts, cw, ch)
                    )

    def row_taps(f, i0, count, *part):
        views = [
            xcols[(f, pl.ds(i0, count), 0, *part)],
            xcols[(f, pl.ds(i0, count), 1, *part)],
            xcols[(f, pl.ds(i0 + 1, count), 0, *part)],
        ]
        return jnp.concatenate([v.reshape(-1, 3 * ch) for v in views], axis=1)

    early = max(1, parts // 2)
    mine = pl.ds(me * per, per)

    def send_map(h, j):
        remote(spat.at[h, j], land.at[h, mine], send1, recv1.at[h], j).start()

    def conv(s, carry):
        q = lax.rem(my_q + 1 + s, q_count)
        devs = pl.ds(q * q_devs, q_devs)
        spread(q)

        @pl.when(s == 0)
        def _():
            fetch[0].wait()

        x = jnp.concatenate([row_taps(f, q * q_rows, q_rows) for f in range(per)], axis=0)
        out = jnp.dot(x, ws_ref[...], preferred_element_type=F32)
        out = out.reshape(per, q_devs, parts, pp, ch).astype(BF16)
        for f in range(per):
            for h in range(parts):
                spat[h, devs, f] = out[f, :, h]

        @pl.when(s == 0)
        def _():
            pl.semaphore_wait(barrier, n - 1)

        @pl.when(s < q_count - 1)
        def _():
            def first(k):
                j = q * q_devs + wrap(me - my_q * q_devs + k, q_devs)
                for h in range(early):
                    send_map(h, j)

            each(0, q_devs, first)

        @pl.when(s == q_count - 1)
        def _():
            def last(k):
                j = q * q_devs + wrap(me - my_q * q_devs + k, q_devs)
                for h in range(early):
                    send_map(h, j)

            each(1, q_devs, last)

        return carry

    lax.fori_loop(0, q_count, conv, 0)

    for h in range(early, parts):
        each(1, n, lambda k: send_map(h, wrap(me + k, n)))
    for h in range(parts):
        pltpu.make_async_copy(spat.at[h, me], land.at[h, mine], recv1.at[h]).start()

    fetch[1].wait()
    fetch[2].wait()

    def clear(t, carry):
        zero = jnp.zeros((t_len, pp, ch), BF16)
        s0[pl.ds(t * t_len, t_len)] = zero
        s1[pl.ds(t * t_len, t_len)] = zero
        d1[pl.ds(length + t * t_len, t_len)] = zero
        d0[pl.ds(length + t * t_len, t_len)] = zero
        return carry

    lax.fori_loop(0, t_count, clear, 0)
    turned_s[...] = jnp.zeros_like(turned_s)
    turned_t[...] = jnp.zeros_like(turned_t)
    sum_s[sp_rows:, :] = jnp.zeros((sum_s.shape[0] - sp_rows, ch), F32)
    for layer in range(layers):
        for tap in range(taps):
            w = wt_ref[layer, tap * ch : (tap + 1) * ch, :]
            wback[layer, tap * ch : (tap + 1) * ch, :] = w.astype(F32).T.astype(BF16)

    def lagged(ref, layer, t0):
        return jnp.concatenate(
            [flat(ref[pl.ds(length + t0 - delay(layer, k), t_len)]) for k in range(taps)], axis=1
        )

    def led(ref, layer, t0):
        return jnp.concatenate(
            [flat(ref[pl.ds(t0 + delay(layer, k), t_len)]) for k in range(taps)], axis=1
        )

    def outer(x, y):
        return lax.dot_general(x, y, (((0,), (0,)), ((), ())), preferred_element_type=F32)

    def steps(count, body):
        if count == 1:
            body(0)
        else:
            lax.fori_loop(0, count, lambda t, c: (body(t), c)[1], 0)

    def temporal(h, carry):
        cols = pl.ds(pl.multiple_of(h * pp, pp), pp)
        drain(land.at[h], recv1.at[h])

        def forward(t):
            t0 = t * t_len
            state = land[h, pl.ds(t0, t_len)]
            s0[pl.ds(length + t0, t_len)] = state
            z = jnp.dot(lagged(s0, 0, t0), wt_ref[0], preferred_element_type=F32)
            act = unflat(jnp.tanh(z))
            act0[pl.ds(t0, t_len)] = act
            state = (state.astype(F32) + act).astype(BF16)
            s1[pl.ds(length + t0, t_len)] = state
            moved = lagged(s1, 1, t0)
            act = unflat(jnp.tanh(jnp.dot(moved, wt_ref[1], preferred_element_type=F32)))
            feat_ref[pl.ds(t0, t_len), cols] = (state.astype(F32) + act).astype(BF16)
            cot = cot_ref[pl.ds(t0, t_len), cols].astype(F32)
            dz = (cot * (1.0 - act * act)).astype(BF16)
            d1[pl.ds(t0, t_len)] = dz
            turned_t[1] += outer(flat(dz), moved)

        steps(t_count, forward)

        def backward(s):
            t0 = (t_count - 1 - s) * t_len
            state = cot_ref[pl.ds(t0, t_len), cols].astype(F32) + unflat(
                jnp.dot(led(d1, 1, t0), wback[1], preferred_element_type=F32)
            )
            act = act0[pl.ds(t0, t_len)]
            dz = (state * (1.0 - act * act)).astype(BF16)
            d0[pl.ds(t0, t_len)] = dz
            state = state + unflat(jnp.dot(led(d0, 0, t0), wback[0], preferred_element_type=F32))
            maps[h, pl.ds(t0, t_len)] = state.astype(BF16)
            turned_t[0] += outer(flat(dz), lagged(s0, 0, t0))

        steps(t_count, backward)

        def send(k):
            j = wrap(me + k, n)
            remote(
                maps.at[h, pl.ds(j * per, per)], back.at[h, me], send2, recv2.at[h], j
            ).start()

        each(1, n, send)
        pltpu.make_async_copy(maps.at[h, mine], back.at[h, me], recv2.at[h]).start()
        return carry

    lax.fori_loop(0, parts, temporal, 0)

    def conv_grad(h):
        drain(back.at[h], recv2.at[h])

        def rows(s):
            i0 = s * g_rows
            x = jnp.concatenate([row_taps(f, i0, g_rows, h) for f in range(per)], axis=0)
            g = [flat(back[h, pl.ds(s * g_devs, g_devs), f]) for f in range(per)]
            turned_s[...] += outer(jnp.concatenate(g, axis=0), x)

        steps(g_count, rows)

    store = pltpu.make_async_copy(feat_ref, feat_hbm, load.at[0])
    store.start()
    for layer in range(layers):
        for k in range(taps):
            at = layer * tap_rows + k * ch
            sum_t[at : at + ch, :] = turned_t[layer, :, k * ch : (k + 1) * ch].T
    red_t.start()
    for h in range(parts):
        conv_grad(h)
        if h == 0:
            red_t.scatter()
    for at in range(0, sp_rows, ch):
        sum_s[at : at + ch, :] = turned_s[:, at : at + ch].T
    red_s.start()
    red_t.gather()
    red_s.scatter()
    red_t.exchange()
    red_s.gather()
    red_t.finish()
    red_s.exchange()
    red_s.finish()

    store.wait()
    red_s.sent()
    red_t.sent()
    for ref, sem in ((land, send1), (back, send2)):
        for h in range(parts):
            drain(spat.at[h, pl.ds(0, n - 1)], sem)


def reduce_scratch(n, size, total_rows, ch):
    groups = n // size
    rows = -(-total_rows // (16 * n)) * 16
    dma = pltpu.SemaphoreType.DMA
    return rows * n, [
        pltpu.VMEM((size, groups, rows, ch), BF16),
        pltpu.VMEM((size, groups, rows, ch), BF16),
        pltpu.VMEM((groups, rows, ch), BF16),
        pltpu.VMEM((groups, rows, ch), BF16),
        pltpu.VMEM((rows, ch), BF16),
        pltpu.VMEM((size, groups, rows, ch), BF16),
        dma((4,)),
        dma((5,)),
    ]


def widen(features, spatial, temporal, sp_rows, tp_rows):
    ch = spatial.shape[1]

    def body(feat_in, s_in, t_in, feat_out, s_out, t_out, feat, s, t, s32, t32, sems):
        loads = [
            pltpu.make_async_copy(src, dst, sems.at[i])
            for i, (src, dst) in enumerate([(feat_in, feat), (s_in, s), (t_in, t)])
        ]
        stores = [
            pltpu.make_async_copy(src, dst, sems.at[3 + i])
            for i, (src, dst) in enumerate([(feat, feat_out), (s32, s_out), (t32, t_out)])
        ]
        for copy in loads:
            copy.start()
        loads[0].wait()
        stores[0].start()
        loads[1].wait()
        s32[...] = s[:sp_rows].astype(F32)
        stores[1].start()
        loads[2].wait()
        t32[...] = t[:tp_rows].astype(F32)
        stores[2].start()
        for copy in stores:
            copy.wait()

    hbm = pl.BlockSpec(memory_space=pltpu.HBM)
    return pl.pallas_call(
        body,
        out_shape=(
            jax.ShapeDtypeStruct(features.shape, BF16),
            jax.ShapeDtypeStruct((sp_rows, ch), F32),
            jax.ShapeDtypeStruct((tp_rows, ch), F32),
        ),
        in_specs=[hbm] * 3,
        out_specs=(hbm,) * 3,
        scratch_shapes=[
            pltpu.VMEM(features.shape, BF16),
            pltpu.VMEM(spatial.shape, BF16),
            pltpu.VMEM(temporal.shape, BF16),
            pltpu.VMEM((sp_rows, ch), F32),
            pltpu.VMEM((tp_rows, ch), F32),
            pltpu.SemaphoreType.DMA((6,)),
        ],
        compiler_params=pltpu.CompilerParams(vmem_limit_bytes=60 * 1024 * 1024),
    )(features, spatial, temporal)


def local(n, frames, w_spatial, w_temporal, dilations, offsets, cotangent):
    per, height, width, ch = frames.shape
    length, pix, _ = cotangent.shape
    layers, taps = offsets.shape
    out_h, out_w = height // 2, width // 2
    sp_rows, tp_rows = 9 * ch, layers * taps * ch
    parts = PARTS if pix == out_w and pix % (16 * PARTS) == 0 else 1
    pp = pix // parts
    pad_s, red_s = reduce_scratch(n, NEAR_S, sp_rows, ch)
    pad_t, red_t = reduce_scratch(n, NEAR_T, tp_rows, ch)
    smem = pl.BlockSpec(memory_space=pltpu.SMEM)
    hbm = pl.BlockSpec(memory_space=pltpu.HBM)
    dma = pltpu.SemaphoreType.DMA
    features, grad_spatial, grad_temporal = pl.pallas_call(
        functools.partial(kernel, n),
        out_shape=(
            jax.ShapeDtypeStruct((length, pix, ch), BF16),
            jax.ShapeDtypeStruct((NEAR_S, n // NEAR_S, pad_s // n, ch), BF16),
            jax.ShapeDtypeStruct((NEAR_T, n // NEAR_T, pad_t // n, ch), BF16),
        ),
        in_specs=[smem, smem, hbm, hbm, hbm, hbm],
        out_specs=(hbm, hbm, hbm),
        scratch_shapes=[
            pltpu.VMEM(cotangent.shape, BF16),
            pltpu.VMEM((4, per, height // 4 + 1, width, ch), BF16),
            pltpu.VMEM((sp_rows, ch), BF16),
            pltpu.VMEM((layers, taps * ch, ch), BF16),
            pltpu.VMEM(cotangent.shape, BF16),
            pltpu.VMEM((per, height // 4 + 1, width + 8, ch), F32),
            pltpu.VMEM((per, out_h + 1, 2, parts, out_w // parts, 3 * ch), BF16),
            pltpu.VMEM((parts, n, per, pp, ch), BF16),
            pltpu.VMEM((parts, length, pp, ch), BF16),
            pltpu.VMEM((2 * length, pp, ch), BF16),
            pltpu.VMEM((2 * length, pp, ch), BF16),
            pltpu.VMEM((length, pp, ch), F32),
            pltpu.VMEM((2 * length, pp, ch), BF16),
            pltpu.VMEM((2 * length, pp, ch), BF16),
            pltpu.VMEM((parts, length, pp, ch), BF16),
            pltpu.VMEM((parts, n, per, pp, ch), BF16),
            pltpu.VMEM((layers, taps * ch, ch), BF16),
            pltpu.VMEM((pad_s, ch), F32),
            pltpu.VMEM((pad_t, ch), F32),
            pltpu.VMEM((ch, sp_rows), F32),
            pltpu.VMEM((layers, ch, taps * ch), F32),
            *red_s,
            *red_t,
            dma,
            dma((parts,)),
            dma,
            dma((parts,)),
            dma((4 + 3,)),
        ],
        compiler_params=pltpu.CompilerParams(
            collective_id=0, has_side_effects=True, vmem_limit_bytes=60 * 1024 * 1024
        ),
        cost_estimate=pl.CostEstimate(
            flops=2 * (length * pix) * ch * ch * 36, bytes_accessed=8 << 20, transcendentals=0
        ),
    )(
        dilations,
        offsets,
        frames,
        w_spatial.reshape(sp_rows, ch),
        w_temporal.reshape(layers, taps * ch, ch),
        cotangent,
    )
    features, grad_spatial, grad_temporal = widen(
        features, grad_spatial.reshape(-1, ch), grad_temporal.reshape(-1, ch), sp_rows, tp_rows
    )
    return (
        features,
        grad_spatial.reshape(3, 3, ch, ch),
        grad_temporal.reshape(layers, taps, ch, ch),
    )


def solution(mesh):
    in_specs = (
        P(("groups", "seq"), None, None, None),
        P(),
        P(),
        P(),
        P(),
        P("groups", "seq", None),
    )
    out_specs = (
        P("groups", "seq", None),
        P("groups", None, None, None),
        P("groups", None, None, None),
    )
    return jax.shard_map(
        functools.partial(local, mesh.shape["seq"]),
        mesh=mesh,
        in_specs=in_specs,
        out_specs=out_specs,
        check_vma=False,
    )
```

```python
import functools

import jax
import jax.numpy as jnp
from jax import lax
from jax.experimental import pallas as pl
from jax.experimental.pallas import tpu as pltpu
from jax.sharding import PartitionSpec as P

BF16 = jnp.bfloat16
F32 = jnp.float32
MESH = pl.DeviceIdType.MESH
PARTS = 2
NEAR_S = 2
NEAR_T = 4


def wrap(x, n):
    return jnp.where(x >= n, x - n, x)


def each(first, end, body):
    if end - first <= 16:
        for k in range(first, end):
            body(k)
    else:
        lax.fori_loop(first, end, lambda k, c: (body(k), c)[1], 0)


def others(n, body):
    half = n // 2
    if n <= 16:
        for k in sorted(range(1, n), key=lambda k: abs(k - half)):
            body(k)
    else:
        lax.fori_loop(0, n - 1, lambda k, c: (body(1 + lax.rem(half - 1 + k, n - 1)), c)[1], 0)


def remote(src, dst, send, recv, to):
    return pltpu.make_async_remote_copy(
        src_ref=src,
        dst_ref=dst,
        send_sem=send,
        recv_sem=recv,
        device_id={"seq": to},
        device_id_type=MESH,
    )


def drain(ref, sem):
    pltpu.make_async_copy(ref, ref, sem).wait()


class Reduce:
    def __init__(self, n, size, out, total, near_out, near_in, far_out, far_in, own, gathered, *sems):
        self.out, self.total, self.near_out, self.near_in = out, total, near_out, near_in
        self.far_out, self.far_in, self.own, self.gathered = far_out, far_in, own, gathered
        self.send, self.recv = sems
        self.size, self.groups = size, n // size
        me = lax.axis_index("seq")
        self.near, self.far = lax.rem(me, size), me // size
        self.rows, self.ch = own.shape
        self.slab = self.groups * self.rows

    def near_loop(self, src_of, dst, hop):
        for k in range(1, self.size):
            c = wrap(self.near + k, self.size)
            to = self.far * self.size + c
            remote(src_of(c), dst, self.send.at[hop], self.recv.at[hop], to).start()

    def far_loop(self, src_of, dst, hop):
        def step(k):
            g = wrap(self.far + k, self.groups)
            to = g * self.size + self.near
            remote(src_of(g), dst, self.send.at[hop], self.recv.at[hop], to).start()

        others(self.groups, step)

    def span(self, c):
        return pl.ds(pl.multiple_of(c * self.slab, self.slab), self.slab)

    def pieces(self, x):
        return x.reshape(self.groups, self.rows, self.ch)

    def start(self):
        for c in range(self.size):
            part = self.total[c * self.slab : (c + 1) * self.slab, :]
            self.near_out[c] = self.pieces(part.astype(BF16))
        self.near_loop(lambda c: self.near_out.at[c], self.near_in.at[self.near], 0)

    def scatter(self):
        mine = self.pieces(self.total[self.span(self.near), :])
        drain(self.near_in.at[pl.ds(0, self.size - 1)], self.recv.at[0])
        for k in range(1, self.size):
            mine = mine + self.near_in[wrap(self.near + k, self.size)].astype(F32)
        self.far_out[...] = mine.astype(BF16)
        dst = self.far_in.at[self.far]
        self.far_loop(lambda g: self.far_out.at[g], dst, 1)
        pltpu.make_async_copy(self.far_out.at[self.far], dst, self.recv.at[1]).start()

    def gather(self):
        drain(self.far_in, self.recv.at[1])
        self.own[...] = jnp.sum(self.far_in[...].astype(F32), axis=0).astype(BF16)
        dst = self.gathered.at[self.near, self.far]
        self.far_loop(lambda g: self.own, dst, 2)
        pltpu.make_async_copy(self.own, dst, self.recv.at[2]).start()

    def exchange(self):
        mine = self.gathered.at[self.near]
        drain(mine, self.recv.at[2])
        self.near_loop(lambda c: mine, mine, 3)
        self.store(self.near)

    def finish(self):
        drain(self.near_in.at[pl.ds(0, self.size - 1)], self.recv.at[3])
        for k in range(1, self.size):
            self.store(wrap(self.near + k, self.size))

    def store(self, c):
        pltpu.make_async_copy(self.gathered.at[c], self.out.at[c], self.recv.at[4]).start()

    def sent(self):
        for hop in (0, 3):
            drain(self.near_in.at[pl.ds(0, self.size - 1)], self.send.at[hop])
        for hop in (1, 2):
            drain(self.far_out.at[pl.ds(0, self.groups - 1)], self.send.at[hop])
        drain(self.gathered, self.recv.at[4])


def kernel(
    n,
    dil_ref,
    off_ref,
    frames_hbm,
    ws_hbm,
    wt_hbm,
    cot_hbm,
    feat_hbm,
    gs_hbm,
    gt_hbm,
    feat_ref,
    frames_ref,
    ws_ref,
    wt_ref,
    cot_ref,
    tmp,
    xcols,
    spat,
    land,
    s0,
    s1,
    act0,
    d1,
    d0,
    maps,
    back,
    wback,
    sum_s,
    sum_t,
    turned_s,
    turned_t,
    *rest,
):
    red_s = Reduce(n, NEAR_S, gs_hbm, sum_s, *rest[0:8])
    red_t = Reduce(n, NEAR_T, gt_hbm, sum_t, *rest[8:16])
    send1, recv1, send2, recv2, load = rest[16:]
    me = lax.axis_index("seq")
    per, height, width, ch = frames_hbm.shape
    length, pix, _ = cot_ref.shape
    layers, taps = off_ref.shape
    parts, _, _, pp, _ = spat.shape
    out_h, out_w = height // 2, width // 2
    cw = out_w // parts
    q_count = 4
    q_rows = out_h // q_count
    q_devs = n // q_count
    t_count = max(1, length * pp // 512)
    t_len = length // t_count
    sp_rows = ws_ref.shape[0]
    tap_rows = taps * ch

    my_q = me // q_devs
    q_in = height // q_count

    def quarter(s):
        step = jnp.where(s == 0, 2, jnp.where(s == 1, 1, jnp.where(s == 2, 3, 0)))
        return wrap(my_q + step, q_count)

    for s in range(q_count):
        q = quarter(s)
        above = jnp.maximum(q * q_in - 1, 0)
        for f in range(per):
            pltpu.make_async_copy(
                frames_hbm.at[f, pl.ds(q * q_in, q_in)],
                frames_ref.at[q, f, pl.ds(1, q_in)],
                load.at[q],
            ).start()
            pltpu.make_async_copy(
                frames_hbm.at[f, pl.ds(above, 1)], frames_ref.at[q, f, pl.ds(0, 1)], load.at[q]
            ).start()
    fetch = [
        pltpu.make_async_copy(a, b, load.at[q_count + i])
        for i, (a, b) in enumerate([(ws_hbm, ws_ref), (wt_hbm, wt_ref), (cot_hbm, cot_ref)])
    ]
    for copy in fetch:
        copy.start()

    def flat(x):
        if pp % 16 == 0:
            return x.reshape(-1, x.shape[-1])
        return x.astype(F32).reshape(-1, x.shape[-1]).astype(BF16)

    def unflat(x):
        return x.reshape(-1, pp, ch)

    def delay(layer, tap):
        return jnp.minimum(off_ref[layer, tap] * dil_ref[layer], length)

    barrier = pltpu.get_barrier_semaphore()

    def greet(s):
        pl.semaphore_signal(
            barrier, inc=1, device_id={"seq": wrap(me + s, n)}, device_id_type=MESH
        )

    each(1, n, greet)

    for f in range(per):
        for g in range(q_in + 1):
            tmp[f, g, 0:8, :] = jnp.zeros((8, ch), F32)

    def spread(q):
        drain(frames_ref.at[q], load.at[q])
        for f in range(per):
            for g in range(q_in + 1):
                row = frames_ref[q, f, g].astype(F32)
                if g == 0:
                    row = jnp.where(q > 0, row, 0.0)
                tmp[f, g, 8 : 8 + width, :] = row
            for g in range(q_in + 1):
                for b in range(3):
                    col = tmp[f, g, pl.ds(7 + b, out_w, stride=2), :].astype(BF16)
                    xcols[f, q * q_rows + g // 2, g % 2, :, :, b * ch : (b + 1) * ch] = (
                        col.reshape(parts, cw, ch)
                    )

    def row_taps(f, i0, count, *part):
        views = [
            xcols[(f, pl.ds(i0, count), 0, *part)],
            xcols[(f, pl.ds(i0, count), 1, *part)],
            xcols[(f, pl.ds(i0 + 1, count), 0, *part)],
        ]
        return jnp.concatenate([v.reshape(-1, 3 * ch) for v in views], axis=1)

    early = max(1, parts // 2)
    mine = pl.ds(me * per, per)

    def send_map(h, j):
        remote(spat.at[h, j], land.at[h, mine], send1, recv1.at[h], j).start()

    def conv(s, carry):
        q = quarter(s)
        devs = pl.ds(q * q_devs, q_devs)
        spread(q)

        @pl.when(s == 0)
        def _():
            fetch[0].wait()

        x = jnp.concatenate([row_taps(f, q * q_rows, q_rows) for f in range(per)], axis=0)
        out = jnp.dot(x, ws_ref[...], preferred_element_type=F32)
        out = out.reshape(per, q_devs, parts, pp, ch).astype(BF16)
        for f in range(per):
            for h in range(parts):
                spat[h, devs, f] = out[f, :, h]

        @pl.when(s == 0)
        def _():
            pl.semaphore_wait(barrier, n - 1)

        @pl.when(s < q_count - 1)
        def _():
            def first(k):
                j = q * q_devs + wrap(me - my_q * q_devs + k, q_devs)
                for h in range(early):
                    send_map(h, j)

            each(0, q_devs, first)

        @pl.when(s == q_count - 1)
        def _():
            def last(k):
                j = q * q_devs + wrap(me - my_q * q_devs + k, q_devs)
                for h in range(early):
                    send_map(h, j)

            each(1, q_devs, last)

        return carry

    lax.fori_loop(0, q_count, conv, 0)

    for h in range(early, parts):
        others(n, lambda k: send_map(h, wrap(me + k, n)))
    for h in range(parts):
        pltpu.make_async_copy(spat.at[h, me], land.at[h, mine], recv1.at[h]).start()

    fetch[1].wait()
    fetch[2].wait()

    def clear(t, carry):
        zero = jnp.zeros((t_len, pp, ch), BF16)
        s0[pl.ds(t * t_len, t_len)] = zero
        s1[pl.ds(t * t_len, t_len)] = zero
        d1[pl.ds(length + t * t_len, t_len)] = zero
        d0[pl.ds(length + t * t_len, t_len)] = zero
        return carry

    lax.fori_loop(0, t_count, clear, 0)
    turned_s[...] = jnp.zeros_like(turned_s)
    turned_t[...] = jnp.zeros_like(turned_t)
    sum_s[sp_rows:, :] = jnp.zeros((sum_s.shape[0] - sp_rows, ch), F32)
    for layer in range(layers):
        for tap in range(taps):
            w = wt_ref[layer, tap * ch : (tap + 1) * ch, :]
            wback[layer, tap * ch : (tap + 1) * ch, :] = w.astype(F32).T.astype(BF16)

    def lagged(ref, layer, t0):
        return jnp.concatenate(
            [flat(ref[pl.ds(length + t0 - delay(layer, k), t_len)]) for k in range(taps)], axis=1
        )

    def led(ref, layer, t0):
        return jnp.concatenate(
            [flat(ref[pl.ds(t0 + delay(layer, k), t_len)]) for k in range(taps)], axis=1
        )

    def outer(x, y):
        return lax.dot_general(x, y, (((0,), (0,)), ((), ())), preferred_element_type=F32)

    def steps(count, body):
        if count == 1:
            body(0)
        else:
            lax.fori_loop(0, count, lambda t, c: (body(t), c)[1], 0)

    def temporal(h, carry):
        cols = pl.ds(pl.multiple_of(h * pp, pp), pp)
        drain(land.at[h], recv1.at[h])

        def forward(t):
            t0 = t * t_len
            state = land[h, pl.ds(t0, t_len)]
            s0[pl.ds(length + t0, t_len)] = state
            z = jnp.dot(lagged(s0, 0, t0), wt_ref[0], preferred_element_type=F32)
            act = unflat(jnp.tanh(z))
            act0[pl.ds(t0, t_len)] = act
            state = (state.astype(F32) + act).astype(BF16)
            s1[pl.ds(length + t0, t_len)] = state
            moved = lagged(s1, 1, t0)
            act = unflat(jnp.tanh(jnp.dot(moved, wt_ref[1], preferred_element_type=F32)))
            feat_ref[pl.ds(t0, t_len), cols] = (state.astype(F32) + act).astype(BF16)
            cot = cot_ref[pl.ds(t0, t_len), cols].astype(F32)
            dz = (cot * (1.0 - act * act)).astype(BF16)
            d1[pl.ds(t0, t_len)] = dz
            turned_t[1] += outer(flat(dz), moved)

        steps(t_count, forward)

        def backward(s):
            t0 = (t_count - 1 - s) * t_len
            state = cot_ref[pl.ds(t0, t_len), cols].astype(F32) + unflat(
                jnp.dot(led(d1, 1, t0), wback[1], preferred_element_type=F32)
            )
            act = act0[pl.ds(t0, t_len)]
            dz = (state * (1.0 - act * act)).astype(BF16)
            d0[pl.ds(t0, t_len)] = dz
            state = state + unflat(jnp.dot(led(d0, 0, t0), wback[0], preferred_element_type=F32))
            maps[h, pl.ds(t0, t_len)] = state.astype(BF16)
            turned_t[0] += outer(flat(dz), lagged(s0, 0, t0))

        steps(t_count, backward)

        def send(k):
            j = wrap(me + k, n)
            remote(
                maps.at[h, pl.ds(j * per, per)], back.at[h, me], send2, recv2.at[h, my_q], j
            ).start()

        others(n, send)
        pltpu.make_async_copy(maps.at[h, mine], back.at[h, me], recv2.at[h, my_q]).start()
        return carry

    lax.fori_loop(0, parts, temporal, 0)

    def conv_grad(h):
        for s in range(q_count):
            q = quarter(s)
            devs = pl.ds(q * q_devs, q_devs)
            drain(back.at[h, devs], recv2.at[h, q])
            x = jnp.concatenate(
                [row_taps(f, q * q_rows, q_rows, h) for f in range(per)], axis=0
            )
            g = jnp.concatenate([flat(back[h, devs, f]) for f in range(per)], axis=0)
            turned_s[...] += outer(g, x)

    store = pltpu.make_async_copy(feat_ref, feat_hbm, load.at[0])
    store.start()
    for layer in range(layers):
        for k in range(taps):
            at = layer * tap_rows + k * ch
            sum_t[at : at + ch, :] = turned_t[layer, :, k * ch : (k + 1) * ch].T
    red_t.start()
    for h in range(parts):
        conv_grad(h)
        if h == 0:
            red_t.scatter()
    for at in range(0, sp_rows, ch):
        sum_s[at : at + ch, :] = turned_s[:, at : at + ch].T
    red_s.start()
    red_t.gather()
    red_s.scatter()
    red_t.exchange()
    red_s.gather()
    red_t.finish()
    red_s.exchange()
    red_s.finish()

    store.wait()
    red_s.sent()
    red_t.sent()
    for ref, sem in ((land, send1), (back, send2)):
        for h in range(parts):
            drain(spat.at[h, pl.ds(0, n - 1)], sem)


def reduce_scratch(n, size, total_rows, ch):
    groups = n // size
    rows = -(-total_rows // (16 * n)) * 16
    dma = pltpu.SemaphoreType.DMA
    return rows * n, [
        pltpu.VMEM((size, groups, rows, ch), BF16),
        pltpu.VMEM((size, groups, rows, ch), BF16),
        pltpu.VMEM((groups, rows, ch), BF16),
        pltpu.VMEM((groups, rows, ch), BF16),
        pltpu.VMEM((rows, ch), BF16),
        pltpu.VMEM((size, groups, rows, ch), BF16),
        dma((4,)),
        dma((5,)),
    ]


def widen(features, spatial, temporal, sp_rows, tp_rows):
    ch = spatial.shape[1]

    def body(feat_in, s_in, t_in, feat_out, s_out, t_out, feat, s, t, s32, t32, sems):
        loads = [
            pltpu.make_async_copy(src, dst, sems.at[i])
            for i, (src, dst) in enumerate([(feat_in, feat), (s_in, s), (t_in, t)])
        ]
        stores = [
            pltpu.make_async_copy(src, dst, sems.at[3 + i])
            for i, (src, dst) in enumerate([(feat, feat_out), (s32, s_out), (t32, t_out)])
        ]
        for copy in loads:
            copy.start()
        loads[0].wait()
        stores[0].start()
        loads[1].wait()
        s32[...] = s[:sp_rows].astype(F32)
        stores[1].start()
        loads[2].wait()
        t32[...] = t[:tp_rows].astype(F32)
        stores[2].start()
        for copy in stores:
            copy.wait()

    hbm = pl.BlockSpec(memory_space=pltpu.HBM)
    return pl.pallas_call(
        body,
        out_shape=(
            jax.ShapeDtypeStruct(features.shape, BF16),
            jax.ShapeDtypeStruct((sp_rows, ch), F32),
            jax.ShapeDtypeStruct((tp_rows, ch), F32),
        ),
        in_specs=[hbm] * 3,
        out_specs=(hbm,) * 3,
        scratch_shapes=[
            pltpu.VMEM(features.shape, BF16),
            pltpu.VMEM(spatial.shape, BF16),
            pltpu.VMEM(temporal.shape, BF16),
            pltpu.VMEM((sp_rows, ch), F32),
            pltpu.VMEM((tp_rows, ch), F32),
            pltpu.SemaphoreType.DMA((6,)),
        ],
        compiler_params=pltpu.CompilerParams(vmem_limit_bytes=60 * 1024 * 1024),
    )(features, spatial, temporal)


def local(n, frames, w_spatial, w_temporal, dilations, offsets, cotangent):
    per, height, width, ch = frames.shape
    length, pix, _ = cotangent.shape
    layers, taps = offsets.shape
    out_h, out_w = height // 2, width // 2
    sp_rows, tp_rows = 9 * ch, layers * taps * ch
    parts = PARTS if pix == out_w and pix % (16 * PARTS) == 0 else 1
    pp = pix // parts
    pad_s, red_s = reduce_scratch(n, NEAR_S, sp_rows, ch)
    pad_t, red_t = reduce_scratch(n, NEAR_T, tp_rows, ch)
    smem = pl.BlockSpec(memory_space=pltpu.SMEM)
    hbm = pl.BlockSpec(memory_space=pltpu.HBM)
    dma = pltpu.SemaphoreType.DMA
    features, grad_spatial, grad_temporal = pl.pallas_call(
        functools.partial(kernel, n),
        out_shape=(
            jax.ShapeDtypeStruct((length, pix, ch), BF16),
            jax.ShapeDtypeStruct((NEAR_S, n // NEAR_S, pad_s // n, ch), BF16),
            jax.ShapeDtypeStruct((NEAR_T, n // NEAR_T, pad_t // n, ch), BF16),
        ),
        in_specs=[smem, smem, hbm, hbm, hbm, hbm],
        out_specs=(hbm, hbm, hbm),
        scratch_shapes=[
            pltpu.VMEM(cotangent.shape, BF16),
            pltpu.VMEM((4, per, height // 4 + 1, width, ch), BF16),
            pltpu.VMEM((sp_rows, ch), BF16),
            pltpu.VMEM((layers, taps * ch, ch), BF16),
            pltpu.VMEM(cotangent.shape, BF16),
            pltpu.VMEM((per, height // 4 + 1, width + 8, ch), F32),
            pltpu.VMEM((per, out_h + 1, 2, parts, out_w // parts, 3 * ch), BF16),
            pltpu.VMEM((parts, n, per, pp, ch), BF16),
            pltpu.VMEM((parts, length, pp, ch), BF16),
            pltpu.VMEM((2 * length, pp, ch), BF16),
            pltpu.VMEM((2 * length, pp, ch), BF16),
            pltpu.VMEM((length, pp, ch), F32),
            pltpu.VMEM((2 * length, pp, ch), BF16),
            pltpu.VMEM((2 * length, pp, ch), BF16),
            pltpu.VMEM((parts, length, pp, ch), BF16),
            pltpu.VMEM((parts, n, per, pp, ch), BF16),
            pltpu.VMEM((layers, taps * ch, ch), BF16),
            pltpu.VMEM((pad_s, ch), F32),
            pltpu.VMEM((pad_t, ch), F32),
            pltpu.VMEM((ch, sp_rows), F32),
            pltpu.VMEM((layers, ch, taps * ch), F32),
            *red_s,
            *red_t,
            dma,
            dma((parts,)),
            dma,
            dma((parts, 4)),
            dma((4 + 3,)),
        ],
        compiler_params=pltpu.CompilerParams(
            collective_id=0, has_side_effects=True, vmem_limit_bytes=60 * 1024 * 1024
        ),
        cost_estimate=pl.CostEstimate(
            flops=2 * (length * pix) * ch * ch * 36, bytes_accessed=8 << 20, transcendentals=0
        ),
    )(
        dilations,
        offsets,
        frames,
        w_spatial.reshape(sp_rows, ch),
        w_temporal.reshape(layers, taps * ch, ch),
        cotangent,
    )
    features, grad_spatial, grad_temporal = widen(
        features, grad_spatial.reshape(-1, ch), grad_temporal.reshape(-1, ch), sp_rows, tp_rows
    )
    return (
        features,
        grad_spatial.reshape(3, 3, ch, ch),
        grad_temporal.reshape(layers, taps, ch, ch),
    )


def solution(mesh):
    in_specs = (
        P(("groups", "seq"), None, None, None),
        P(),
        P(),
        P(),
        P(),
        P("groups", "seq", None),
    )
    out_specs = (
        P("groups", "seq", None),
        P("groups", None, None, None),
        P("groups", None, None, None),
    )
    return jax.shard_map(
        functools.partial(local, mesh.shape["seq"]),
        mesh=mesh,
        in_specs=in_specs,
        out_specs=out_specs,
        check_vma=False,
    )
```

```python
import functools

import jax
import jax.numpy as jnp
from jax import lax
from jax.experimental import pallas as pl
from jax.experimental.pallas import tpu as pltpu
from jax.sharding import PartitionSpec as P

BF16 = jnp.bfloat16
F32 = jnp.float32
MESH = pl.DeviceIdType.MESH
PARTS = 2
NEAR_S = 2
NEAR_T = 4


def wrap(x, n):
    return jnp.where(x >= n, x - n, x)


def each(first, end, body):
    if end - first <= 16:
        for k in range(first, end):
            body(k)
    else:
        lax.fori_loop(first, end, lambda k, c: (body(k), c)[1], 0)


def remote(src, dst, send, recv, to):
    return pltpu.make_async_remote_copy(
        src_ref=src,
        dst_ref=dst,
        send_sem=send,
        recv_sem=recv,
        device_id={"seq": to},
        device_id_type=MESH,
    )


def drain(ref, sem):
    pltpu.make_async_copy(ref, ref, sem).wait()


class Reduce:
    def __init__(self, n, size, out, total, near_out, near_in, far_out, far_in, own, gathered, *sems):
        self.out, self.total, self.near_out, self.near_in = out, total, near_out, near_in
        self.far_out, self.far_in, self.own, self.gathered = far_out, far_in, own, gathered
        self.send, self.recv = sems
        self.size, self.groups = size, n // size
        me = lax.axis_index("seq")
        self.near, self.far = lax.rem(me, size), me // size
        self.rows, self.ch = own.shape
        self.slab = self.groups * self.rows

    def near_loop(self, src_of, dst, hop):
        for k in range(1, self.size):
            c = wrap(self.near + k, self.size)
            to = self.far * self.size + c
            remote(src_of(c), dst, self.send.at[hop], self.recv.at[hop], to).start()

    def far_loop(self, src_of, dst, hop):
        def step(k):
            g = wrap(self.far + k, self.groups)
            to = g * self.size + self.near
            remote(src_of(g), dst, self.send.at[hop], self.recv.at[hop], to).start()

        each(1, self.groups, step)

    def span(self, c):
        return pl.ds(pl.multiple_of(c * self.slab, self.slab), self.slab)

    def pieces(self, x):
        return x.reshape(self.groups, self.rows, self.ch)

    def start(self):
        for c in range(self.size):
            part = self.total[c * self.slab : (c + 1) * self.slab, :]
            self.near_out[c] = self.pieces(part.astype(BF16))
        self.near_loop(lambda c: self.near_out.at[c], self.near_in.at[self.near], 0)

    def scatter(self):
        mine = self.pieces(self.total[self.span(self.near), :])
        drain(self.near_in.at[pl.ds(0, self.size - 1)], self.recv.at[0])
        for k in range(1, self.size):
            mine = mine + self.near_in[wrap(self.near + k, self.size)].astype(F32)
        self.far_out[...] = mine.astype(BF16)
        dst = self.far_in.at[self.far]
        self.far_loop(lambda g: self.far_out.at[g], dst, 1)
        pltpu.make_async_copy(self.far_out.at[self.far], dst, self.recv.at[1]).start()

    def gather(self):
        drain(self.far_in, self.recv.at[1])
        self.own[...] = jnp.sum(self.far_in[...].astype(F32), axis=0).astype(BF16)
        dst = self.gathered.at[self.near, self.far]
        self.far_loop(lambda g: self.own, dst, 2)
        pltpu.make_async_copy(self.own, dst, self.recv.at[2]).start()

    def exchange(self):
        mine = self.gathered.at[self.near]
        drain(mine, self.recv.at[2])
        self.near_loop(lambda c: mine, mine, 3)
        self.store(self.near)

    def finish(self):
        drain(self.near_in.at[pl.ds(0, self.size - 1)], self.recv.at[3])
        for k in range(1, self.size):
            self.store(wrap(self.near + k, self.size))

    def store(self, c):
        pltpu.make_async_copy(self.gathered.at[c], self.out.at[c], self.recv.at[4]).start()

    def sent(self):
        for hop in (0, 3):
            drain(self.near_in.at[pl.ds(0, self.size - 1)], self.send.at[hop])
        for hop in (1, 2):
            drain(self.far_out.at[pl.ds(0, self.groups - 1)], self.send.at[hop])
        drain(self.gathered, self.recv.at[4])


def kernel(
    n,
    dil_ref,
    off_ref,
    frames_hbm,
    ws_hbm,
    wt_hbm,
    cot_hbm,
    feat_hbm,
    gs_hbm,
    gt_hbm,
    feat_ref,
    frames_ref,
    ws_ref,
    wt_ref,
    cot_ref,
    tmp,
    xcols,
    spat,
    land,
    s0,
    s1,
    act0,
    d1,
    d0,
    maps,
    back,
    wback,
    sum_s,
    sum_t,
    turned_s,
    turned_t,
    *rest,
):
    red_s = Reduce(n, NEAR_S, gs_hbm, sum_s, *rest[0:8])
    red_t = Reduce(n, NEAR_T, gt_hbm, sum_t, *rest[8:16])
    send1, recv1, send2, recv2, load = rest[16:]
    me = lax.axis_index("seq")
    per, height, width, ch = frames_hbm.shape
    length, pix, _ = cot_ref.shape
    layers, taps = off_ref.shape
    parts, _, _, pp, _ = spat.shape
    out_h, out_w = height // 2, width // 2
    cw = out_w // parts
    q_count = 4
    q_rows = out_h // q_count
    q_devs = n // q_count
    g_count = max(1, per * out_h * cw // 512)
    g_rows, g_devs = out_h // g_count, n // g_count
    t_count = max(1, length * pp // 512)
    t_len = length // t_count
    sp_rows = ws_ref.shape[0]
    tap_rows = taps * ch

    my_q = me // q_devs
    q_in = height // q_count

    for s in range(q_count):
        q = lax.rem(my_q + 1 + s, q_count)
        above = jnp.maximum(q * q_in - 1, 0)
        for f in range(per):
            pltpu.make_async_copy(
                frames_hbm.at[f, pl.ds(q * q_in, q_in)],
                frames_ref.at[q, f, pl.ds(1, q_in)],
                load.at[q],
            ).start()
            pltpu.make_async_copy(
                frames_hbm.at[f, pl.ds(above, 1)], frames_ref.at[q, f, pl.ds(0, 1)], load.at[q]
            ).start()
    fetch = [
        pltpu.make_async_copy(a, b, load.at[q_count + i])
        for i, (a, b) in enumerate([(ws_hbm, ws_ref), (wt_hbm, wt_ref), (cot_hbm, cot_ref)])
    ]
    for copy in fetch:
        copy.start()

    def flat(x):
        if pp % 16 == 0:
            return x.reshape(-1, x.shape[-1])
        return x.astype(F32).reshape(-1, x.shape[-1]).astype(BF16)

    def unflat(x):
        return x.reshape(-1, pp, ch)

    def delay(layer, tap):
        return jnp.minimum(off_ref[layer, tap] * dil_ref[layer], length)

    barrier = pltpu.get_barrier_semaphore()

    def greet(s):
        pl.semaphore_signal(
            barrier, inc=1, device_id={"seq": wrap(me + s, n)}, device_id_type=MESH
        )

    each(1, n, greet)

    for f in range(per):
        for g in range(q_in + 1):
            tmp[f, g, 0:8, :] = jnp.zeros((8, ch), F32)

    def spread(q):
        drain(frames_ref.at[q], load.at[q])
        for f in range(per):
            for g in range(q_in + 1):
                row = frames_ref[q, f, g].astype(F32)
                if g == 0:
                    row = jnp.where(q > 0, row, 0.0)
                tmp[f, g, 8 : 8 + width, :] = row
            for g in range(q_in + 1):
                for b in range(3):
                    col = tmp[f, g, pl.ds(7 + b, out_w, stride=2), :].astype(BF16)
                    xcols[f, q * q_rows + g // 2, g % 2, :, :, b * ch : (b + 1) * ch] = (
                        col.reshape(parts, cw, ch)
                    )

    def row_taps(f, i0, count, *part):
        views = [
            xcols[(f, pl.ds(i0, count), 0, *part)],
            xcols[(f, pl.ds(i0, count), 1, *part)],
            xcols[(f, pl.ds(i0 + 1, count), 0, *part)],
        ]
        return jnp.concatenate([v.reshape(-1, 3 * ch) for v in views], axis=1)

    early = max(1, parts // 2)
    mine = pl.ds(me * per, per)

    def send_map(h, j):
        remote(spat.at[h, j], land.at[h, mine], send1, recv1.at[h], j).start()

    def conv(s, carry):
        q = lax.rem(my_q + 1 + s, q_count)
        devs = pl.ds(q * q_devs, q_devs)
        spread(q)

        @pl.when(s == 0)
        def _():
            fetch[0].wait()

        x = jnp.concatenate([row_taps(f, q * q_rows, q_rows) for f in range(per)], axis=0)
        out = jnp.dot(x, ws_ref[...], preferred_element_type=F32)
        out = out.reshape(per, q_devs, parts, pp, ch).astype(BF16)
        for f in range(per):
            for h in range(parts):
                spat[h, devs, f] = out[f, :, h]

        @pl.when(s == 0)
        def _():
            pl.semaphore_wait(barrier, n - 1)

        @pl.when(s < q_count - 1)
        def _():
            def first(k):
                j = q * q_devs + wrap(me - my_q * q_devs + k, q_devs)
                for h in range(early):
                    send_map(h, j)

            each(0, q_devs, first)

        @pl.when(s == q_count - 1)
        def _():
            def last(k):
                j = q * q_devs + wrap(me - my_q * q_devs + k, q_devs)
                for h in range(early):
                    send_map(h, j)

            each(1, q_devs, last)

        return carry

    lax.fori_loop(0, q_count, conv, 0)

    for h in range(early, parts):
        each(1, n, lambda k: send_map(h, wrap(me + k, n)))
    for h in range(parts):
        pltpu.make_async_copy(spat.at[h, me], land.at[h, mine], recv1.at[h]).start()

    fetch[1].wait()
    fetch[2].wait()

    def clear(i, carry):
        h, t = i // t_count, lax.rem(i, t_count)
        zero = jnp.zeros((t_len, pp, ch), BF16)
        s0[h, pl.ds(t * t_len, t_len)] = zero
        s1[h, pl.ds(t * t_len, t_len)] = zero
        d1[h, pl.ds(length + t * t_len, t_len)] = zero
        d0[h, pl.ds(length + t * t_len, t_len)] = zero
        return carry

    lax.fori_loop(0, parts * t_count, clear, 0)
    turned_s[...] = jnp.zeros_like(turned_s)
    turned_t[...] = jnp.zeros_like(turned_t)
    sum_s[sp_rows:, :] = jnp.zeros((sum_s.shape[0] - sp_rows, ch), F32)
    for layer in range(layers):
        for tap in range(taps):
            w = wt_ref[layer, tap * ch : (tap + 1) * ch, :]
            wback[layer, tap * ch : (tap + 1) * ch, :] = w.astype(F32).T.astype(BF16)

    def lagged(ref, layer, t0):
        return jnp.concatenate(
            [flat(ref[pl.ds(length + t0 - delay(layer, k), t_len)]) for k in range(taps)], axis=1
        )

    def led(ref, layer, t0):
        return jnp.concatenate(
            [flat(ref[pl.ds(t0 + delay(layer, k), t_len)]) for k in range(taps)], axis=1
        )

    def outer(x, y):
        return lax.dot_general(x, y, (((0,), (0,)), ((), ())), preferred_element_type=F32)

    def steps(count, body):
        if count == 1:
            body(0)
        else:
            lax.fori_loop(0, count, lambda t, c: (body(t), c)[1], 0)

    def temporal(h, carry):
        cols = pl.ds(pl.multiple_of(h * pp, pp), pp)
        drain(land.at[h], recv1.at[h])

        def forward(t):
            t0 = t * t_len
            state = land[h, pl.ds(t0, t_len)]
            s0[h, pl.ds(length + t0, t_len)] = state
            z = jnp.dot(lagged(s0.at[h], 0, t0), wt_ref[0], preferred_element_type=F32)
            act = unflat(jnp.tanh(z))
            act0[pl.ds(t0, t_len)] = act
            state = (state.astype(F32) + act).astype(BF16)
            s1[h, pl.ds(length + t0, t_len)] = state
            z = jnp.dot(lagged(s1.at[h], 1, t0), wt_ref[1], preferred_element_type=F32)
            act = unflat(jnp.tanh(z))
            feat_ref[pl.ds(t0, t_len), cols] = (state.astype(F32) + act).astype(BF16)
            cot = cot_ref[pl.ds(t0, t_len), cols].astype(F32)
            dz = (cot * (1.0 - act * act)).astype(BF16)
            d1[h, pl.ds(t0, t_len)] = dz

        steps(t_count, forward)

        def backward(s):
            t0 = (t_count - 1 - s) * t_len
            state = cot_ref[pl.ds(t0, t_len), cols].astype(F32) + unflat(
                jnp.dot(led(d1.at[h], 1, t0), wback[1], preferred_element_type=F32)
            )
            act = act0[pl.ds(t0, t_len)]
            dz = (state * (1.0 - act * act)).astype(BF16)
            d0[h, pl.ds(t0, t_len)] = dz
            state = state + unflat(jnp.dot(led(d0.at[h], 0, t0), wback[0], preferred_element_type=F32))
            maps[h, pl.ds(t0, t_len)] = state.astype(BF16)

        steps(t_count, backward)

        def send(k):
            j = wrap(me + k, n)
            remote(
                maps.at[h, pl.ds(j * per, per)], back.at[h, me], send2, recv2.at[h], j
            ).start()

        each(1, n, send)
        pltpu.make_async_copy(maps.at[h, mine], back.at[h, me], recv2.at[h]).start()
        return carry

    lax.fori_loop(0, parts, temporal, 0)

    def temporal_grad(i, carry):
        h, t0 = i // t_count, lax.rem(i, t_count) * t_len
        turned_t[1] += outer(flat(d1[h, pl.ds(t0, t_len)]), lagged(s1.at[h], 1, t0))
        turned_t[0] += outer(flat(d0[h, pl.ds(t0, t_len)]), lagged(s0.at[h], 0, t0))
        return carry

    lax.fori_loop(0, parts * t_count, temporal_grad, 0)

    def conv_grad(h):
        drain(back.at[h], recv2.at[h])

        def rows(s):
            i0 = s * g_rows
            x = jnp.concatenate([row_taps(f, i0, g_rows, h) for f in range(per)], axis=0)
            g = [flat(back[h, pl.ds(s * g_devs, g_devs), f]) for f in range(per)]
            turned_s[...] += outer(jnp.concatenate(g, axis=0), x)

        steps(g_count, rows)

    store = pltpu.make_async_copy(feat_ref, feat_hbm, load.at[0])
    store.start()
    for layer in range(layers):
        for k in range(taps):
            at = layer * tap_rows + k * ch
            sum_t[at : at + ch, :] = turned_t[layer, :, k * ch : (k + 1) * ch].T
    red_t.start()
    for h in range(parts):
        conv_grad(h)
        if h == 0:
            red_t.scatter()
    for at in range(0, sp_rows, ch):
        sum_s[at : at + ch, :] = turned_s[:, at : at + ch].T
    red_s.start()
    red_t.gather()
    red_s.scatter()
    red_t.exchange()
    red_s.gather()
    red_t.finish()
    red_s.exchange()
    red_s.finish()

    store.wait()
    red_s.sent()
    red_t.sent()
    for ref, sem in ((land, send1), (back, send2)):
        for h in range(parts):
            drain(spat.at[h, pl.ds(0, n - 1)], sem)


def reduce_scratch(n, size, total_rows, ch):
    groups = n // size
    rows = -(-total_rows // (16 * n)) * 16
    dma = pltpu.SemaphoreType.DMA
    return rows * n, [
        pltpu.VMEM((size, groups, rows, ch), BF16),
        pltpu.VMEM((size, groups, rows, ch), BF16),
        pltpu.VMEM((groups, rows, ch), BF16),
        pltpu.VMEM((groups, rows, ch), BF16),
        pltpu.VMEM((rows, ch), BF16),
        pltpu.VMEM((size, groups, rows, ch), BF16),
        dma((4,)),
        dma((5,)),
    ]


def widen(features, spatial, temporal, sp_rows, tp_rows):
    ch = spatial.shape[1]

    def body(feat_in, s_in, t_in, feat_out, s_out, t_out, feat, s, t, s32, t32, sems):
        loads = [
            pltpu.make_async_copy(src, dst, sems.at[i])
            for i, (src, dst) in enumerate([(feat_in, feat), (s_in, s), (t_in, t)])
        ]
        stores = [
            pltpu.make_async_copy(src, dst, sems.at[3 + i])
            for i, (src, dst) in enumerate([(feat, feat_out), (s32, s_out), (t32, t_out)])
        ]
        for copy in loads:
            copy.start()
        loads[0].wait()
        stores[0].start()
        loads[1].wait()
        s32[...] = s[:sp_rows].astype(F32)
        stores[1].start()
        loads[2].wait()
        t32[...] = t[:tp_rows].astype(F32)
        stores[2].start()
        for copy in stores:
            copy.wait()

    hbm = pl.BlockSpec(memory_space=pltpu.HBM)
    return pl.pallas_call(
        body,
        out_shape=(
            jax.ShapeDtypeStruct(features.shape, BF16),
            jax.ShapeDtypeStruct((sp_rows, ch), F32),
            jax.ShapeDtypeStruct((tp_rows, ch), F32),
        ),
        in_specs=[hbm] * 3,
        out_specs=(hbm,) * 3,
        scratch_shapes=[
            pltpu.VMEM(features.shape, BF16),
            pltpu.VMEM(spatial.shape, BF16),
            pltpu.VMEM(temporal.shape, BF16),
            pltpu.VMEM((sp_rows, ch), F32),
            pltpu.VMEM((tp_rows, ch), F32),
            pltpu.SemaphoreType.DMA((6,)),
        ],
        compiler_params=pltpu.CompilerParams(vmem_limit_bytes=60 * 1024 * 1024),
    )(features, spatial, temporal)


def local(n, frames, w_spatial, w_temporal, dilations, offsets, cotangent):
    per, height, width, ch = frames.shape
    length, pix, _ = cotangent.shape
    layers, taps = offsets.shape
    out_h, out_w = height // 2, width // 2
    sp_rows, tp_rows = 9 * ch, layers * taps * ch
    parts = PARTS if pix == out_w and pix % (16 * PARTS) == 0 else 1
    pp = pix // parts
    pad_s, red_s = reduce_scratch(n, NEAR_S, sp_rows, ch)
    pad_t, red_t = reduce_scratch(n, NEAR_T, tp_rows, ch)
    smem = pl.BlockSpec(memory_space=pltpu.SMEM)
    hbm = pl.BlockSpec(memory_space=pltpu.HBM)
    dma = pltpu.SemaphoreType.DMA
    features, grad_spatial, grad_temporal = pl.pallas_call(
        functools.partial(kernel, n),
        out_shape=(
            jax.ShapeDtypeStruct((length, pix, ch), BF16),
            jax.ShapeDtypeStruct((NEAR_S, n // NEAR_S, pad_s // n, ch), BF16),
            jax.ShapeDtypeStruct((NEAR_T, n // NEAR_T, pad_t // n, ch), BF16),
        ),
        in_specs=[smem, smem, hbm, hbm, hbm, hbm],
        out_specs=(hbm, hbm, hbm),
        scratch_shapes=[
            pltpu.VMEM(cotangent.shape, BF16),
            pltpu.VMEM((4, per, height // 4 + 1, width, ch), BF16),
            pltpu.VMEM((sp_rows, ch), BF16),
            pltpu.VMEM((layers, taps * ch, ch), BF16),
            pltpu.VMEM(cotangent.shape, BF16),
            pltpu.VMEM((per, height // 4 + 1, width + 8, ch), F32),
            pltpu.VMEM((per, out_h + 1, 2, parts, out_w // parts, 3 * ch), BF16),
            pltpu.VMEM((parts, n, per, pp, ch), BF16),
            pltpu.VMEM((parts, length, pp, ch), BF16),
            pltpu.VMEM((parts, 2 * length, pp, ch), BF16),
            pltpu.VMEM((parts, 2 * length, pp, ch), BF16),
            pltpu.VMEM((length, pp, ch), F32),
            pltpu.VMEM((parts, 2 * length, pp, ch), BF16),
            pltpu.VMEM((parts, 2 * length, pp, ch), BF16),
            pltpu.VMEM((parts, length, pp, ch), BF16),
            pltpu.VMEM((parts, n, per, pp, ch), BF16),
            pltpu.VMEM((layers, taps * ch, ch), BF16),
            pltpu.VMEM((pad_s, ch), F32),
            pltpu.VMEM((pad_t, ch), F32),
            pltpu.VMEM((ch, sp_rows), F32),
            pltpu.VMEM((layers, ch, taps * ch), F32),
            *red_s,
            *red_t,
            dma,
            dma((parts,)),
            dma,
            dma((parts,)),
            dma((4 + 3,)),
        ],
        compiler_params=pltpu.CompilerParams(
            collective_id=0, has_side_effects=True, vmem_limit_bytes=60 * 1024 * 1024
        ),
        cost_estimate=pl.CostEstimate(
            flops=2 * (length * pix) * ch * ch * 36, bytes_accessed=8 << 20, transcendentals=0
        ),
    )(
        dilations,
        offsets,
        frames,
        w_spatial.reshape(sp_rows, ch),
        w_temporal.reshape(layers, taps * ch, ch),
        cotangent,
    )
    features, grad_spatial, grad_temporal = widen(
        features, grad_spatial.reshape(-1, ch), grad_temporal.reshape(-1, ch), sp_rows, tp_rows
    )
    return (
        features,
        grad_spatial.reshape(3, 3, ch, ch),
        grad_temporal.reshape(layers, taps, ch, ch),
    )


def solution(mesh):
    in_specs = (
        P(("groups", "seq"), None, None, None),
        P(),
        P(),
        P(),
        P(),
        P("groups", "seq", None),
    )
    out_specs = (
        P("groups", "seq", None),
        P("groups", None, None, None),
        P("groups", None, None, None),
    )
    return jax.shard_map(
        functools.partial(local, mesh.shape["seq"]),
        mesh=mesh,
        in_specs=in_specs,
        out_specs=out_specs,
        check_vma=False,
    )
```
